128 devices in a mesh: row: 8 (over x, core), col: 16 (over y, z).
Axes of the slice: x: 4, y: 4, z: 4, core: 2. Of those that a mesh axis runs over, the one named last changes fastest.
Arguments:
- nodes: bfloat16 [8192, 512], P(('row', 'col')), may hold values from -6 to 6
- edges: bfloat16 [8, 16, 4096, 512], P('row', 'col'), may hold values from -6 to 6
- senders: int32 [8, 16, 4096], P('row', 'col'), may hold values from 0 to 511
- receivers: int32 [8, 16, 4096], P('row', 'col'), may hold values from 0 to 1023
- levels: int32 [8, 16, 4096], P('row', 'col'), may hold values from 0 to 6
- counts: int32 [8, 16], P('row', 'col'), may hold values from 1 to 4096, as said below
- edge_w1: bfloat16 [3, 512, 512], replicated, may hold values from -0.15625 to 0.15625
- level_bias: bfloat16 [7, 512], replicated, may hold values from -6 to 6
- edge_w2: bfloat16 [512, 512], replicated, may hold values from -0.25 to 0.25
- edge_gain: float32 [512], replicated, may hold values from 0.1 to 1.9
- node_w1: bfloat16 [2, 512, 512], replicated, may hold values from -0.1875 to 0.1875
- node_w2: bfloat16 [512, 512], replicated, may hold values from -0.25 to 0.25
- node_gain: float32 [512], replicated, may hold values from 0.1 to 1.9
- grid: bfloat16 [131072, 512], P(('row', 'col')), may hold values from -6 to 6
- send_rows: int32 [128, 128, 4], P(('row', 'col')), may hold values from 0 to 63, as said below
- dec_index: int32 [131072, 3], P(('row', 'col')), may hold values from 0 to 511, as said below
- dec_w1: bfloat16 [2, 512, 512], replicated, may hold values from -0.1875 to 0.1875
- dec_w2: bfloat16 [512, 512], replicated, may hold values from -0.25 to 0.25
- dec_gain: float32 [512], replicated, may hold values from 0.1 to 1.9
Outputs:
- nodes_out: bfloat16 [8192, 512], P(('row', 'col'))
- edges_out: bfloat16 [8, 16, 4096, 512], P('row', 'col')
- grid_out: bfloat16 [131072, 512], P(('row', 'col'))
The draws below stay inside these ranges and needn't reach their ends.
Inputs may be any that keep to these rules, and one draw needn't show every extreme that they name: `senders`: at slots at or beyond the tile's count the index is arbitrary and unused. `receivers`: at slots at or beyond the tile's count the index is arbitrary and unused. `counts`: some tile is full in every draw. `send_rows`: the 4 rows that one device sends to one band device are distinct. `dec_index`: buffer rows are laid out by source device, then slot; every row of a band's buffer is named by some decoder edge of that band.
All inputs are finite; a program needn't handle non-finite values.
Results may differ from the reference program's by a relative error of at most 0.015.
Values may be sent and summed in bfloat16 or wider, within the bound.
No kernel may reach another device: no remote copies, remote signals or barrier semaphores. Data moves between devices by JAX's collectives and lax.ppermute only.
A program may use at most 128 MiB of HBM per device.

```python
import jax
import jax.numpy as jnp
from jax import lax

D = 512
LEVELS = 7
KD = 3
NB = 64
RQ = 4
GC = 1024
NODES = 8192
EC = 4096
GRID = 131072
N_ROW = 8
N_COL = 16


def draw_counts(key, part):
    key_spread, key_pick = jax.random.split(jax.random.fold_in(key, 11))
    spread = jax.random.randint(key_spread, (N_ROW, N_COL), 300, 1001)
    filled = spread * spread // 1000 * EC // 1000
    filled = jnp.maximum(filled, 1).reshape(-1)
    chosen = jax.random.randint(key_pick, (), 0, N_ROW * N_COL)
    filled = jnp.where(jnp.arange(N_ROW * N_COL) == chosen, EC, filled)
    return filled.reshape(N_ROW, N_COL).astype(jnp.int32)


def draw_send_rows(key, part):
    device_count = N_ROW * N_COL
    scores = jax.random.randint(jax.random.fold_in(key, 12), (device_count, device_count, NB), 0, 2 ** 20)
    scores = scores * NB + jnp.arange(NB, dtype=jnp.int32)
    values_top, chosen = lax.top_k(scores, RQ)
    return chosen.astype(jnp.int32)


def draw_dec_index(key, part):
    device_count = N_ROW * N_COL
    keys = jax.random.split(jax.random.fold_in(key, 13), device_count)
    orders = jax.vmap(lambda single_key: jax.random.permutation(single_key, GC * KD))(keys)
    return (orders % (device_count * RQ)).reshape(device_count * GC, KD).astype(jnp.int32)


def set_ends(entries, rng, least, top_value):
    longest = entries.shape.index(max(entries.shape))
    spots = []
    for shift in (0, 1):
        where = [jax.random.randint(jax.random.fold_in(rng, axis), (), 0, length) for axis, length in enumerate(entries.shape)]
        where[longest] = (where[longest] + shift) % entries.shape[longest]
        spots.append(tuple(where))
    return entries.at[spots[0]].set(least).at[spots[1]].set(top_value)


def block_levels(key, extent, cuts, low, largest):
    factor_of, own = 1.0, jax.random.fold_in(key, 6)
    for position, shards_of in cuts:
        steps = jnp.exp(jax.random.uniform(jax.random.fold_in(own, position), (shards_of,), jnp.float32, low / len(cuts), largest / len(cuts)))
        factor_of = factor_of * jnp.repeat(steps, extent[position] // shards_of).reshape([-1 if axis == position else 1 for axis in range(len(extent))])
    return factor_of


def bell_draw(rng, shape, scale, most, cuts=(), kind=jnp.bfloat16):
    result = jax.random.normal(rng, shape, jnp.float32) * scale
    if len(cuts) > 0:
        result = block_levels(rng, shape, cuts, -0.22, 0.18) * result
    return jnp.clip(result, min=-most, max=most).astype(kind)


def setup_inputs(seed: int = 0) -> dict:
    key_list = jax.random.split(jax.random.key(seed), 20)
    return {
        "nodes": bell_draw(key_list[0], (NODES, D), 1.0, 6.0, ((0, 128),)),
        "edges": bell_draw(key_list[1], (N_ROW, N_COL, EC, D), 1.0, 6.0, ((0, 8), (1, 16))),
        "senders": set_ends(jax.random.randint(key_list[2], (N_ROW, N_COL, EC), 0, NODES // N_COL), jax.random.fold_in(key_list[2], 1), 0, (NODES // N_COL) - 1).astype(jnp.int32),
        "receivers": set_ends(jax.random.randint(key_list[3], (N_ROW, N_COL, EC), 0, NODES // N_ROW), jax.random.fold_in(key_list[3], 1), 0, (NODES // N_ROW) - 1).astype(jnp.int32),
        "levels": set_ends(jax.random.randint(key_list[4], (N_ROW, N_COL, EC), 0, LEVELS), jax.random.fold_in(key_list[4], 1), 0, LEVELS - 1).astype(jnp.int32),
        "counts": draw_counts(jax.random.fold_in(key_list[19], 71), 0),
        "edge_w1": bell_draw(key_list[6], (3, D, D), (3 * D) ** -0.5, 0.15625),
        "level_bias": bell_draw(key_list[7], (LEVELS, D), 1.0, 6.0),
        "edge_w2": bell_draw(key_list[8], (D, D), D ** -0.5, 0.25),
        "edge_gain": jnp.clip(1.0 + 0.18 * jax.random.normal(key_list[9], (D,), jnp.float32), 0.1, 1.9),
        "node_w1": bell_draw(key_list[10], (2, D, D), (2 * D) ** -0.5, 0.1875),
        "node_w2": bell_draw(key_list[11], (D, D), D ** -0.5, 0.25),
        "node_gain": jnp.clip(1.0 + 0.18 * jax.random.normal(key_list[12], (D,), jnp.float32), 0.1, 1.9),
        "grid": bell_draw(key_list[13], (GRID, D), 1.0, 6.0, ((0, 128),)),
        "send_rows": draw_send_rows(jax.random.fold_in(key_list[19], 71), 0),
        "dec_index": draw_dec_index(jax.random.fold_in(key_list[19], 71), 0),
        "dec_w1": bell_draw(key_list[16], (2, D, D), (2 * D) ** -0.5, 0.1875),
        "dec_w2": bell_draw(key_list[17], (D, D), D ** -0.5, 0.25),
        "dec_gain": jnp.clip(1.0 + 0.18 * jax.random.normal(key_list[18], (D,), jnp.float32), 0.1, 1.9),
    }


EPSILON = 1e-05

def layer_norm(values, gain):
    center = values - lax.optimization_barrier(jnp.mean(values, axis=-1, keepdims=True))
    spread = lax.optimization_barrier(jnp.mean(center * center, axis=-1, keepdims=True))
    return center * lax.rsqrt(spread + EPSILON) * gain

def mlp_tail(pre, second_weight, gain):
    hidden = jax.nn.silu(pre).astype(jnp.bfloat16)
    output = jnp.dot(hidden, second_weight, preferred_element_type=jnp.float32)
    return layer_norm(output, gain)

def reference(nodes, edges, senders, receivers, levels, counts, edge_w1, level_bias, edge_w2, edge_gain, node_w1, node_w2, node_gain, grid, send_rows, dec_index, dec_w1, dec_w2, dec_gain):
    tiles = N_ROW * N_COL
    block = NODES // tiles
    recv_span = NODES // N_ROW
    row_ids = jnp.arange(N_ROW, dtype=jnp.int32)[:, None, None]
    col_ids = jnp.arange(N_COL, dtype=jnp.int32)[None, :, None]
    sender_global = senders // block * (N_COL * block) + col_ids * block + senders % block
    receiver_global = row_ids * recv_span + receivers
    valid = jnp.arange(EC, dtype=jnp.int32)[None, None, :] < counts[:, :, None]
    sender_proj = jnp.dot(nodes, edge_w1[1], preferred_element_type=jnp.float32)
    receiver_proj = jnp.dot(nodes, edge_w1[2], preferred_element_type=jnp.float32)
    level_range = jnp.arange(LEVELS, dtype=jnp.int32)

    def tile_step(total, item):
        edge_rows, send_ids, recv_ids, level_ids, used = item
        onehot = (level_ids[:, None] == level_range[None, :]).astype(jnp.bfloat16)
        pre = jnp.dot(edge_rows, edge_w1[0], preferred_element_type=jnp.float32)
        pre = pre + sender_proj[send_ids] + receiver_proj[recv_ids]
        pre = pre + jnp.dot(onehot, level_bias, preferred_element_type=jnp.float32)
        message = mlp_tail(pre, edge_w2, edge_gain).astype(jnp.bfloat16)
        kept = jnp.where(used[:, None], message.astype(jnp.float32), jnp.zeros((), jnp.float32))
        updated = (edge_rows.astype(jnp.float32) + kept).astype(jnp.bfloat16)
        return (total.at[recv_ids].add(kept), updated)
    items = (edges.reshape(tiles, EC, D), sender_global.reshape(tiles, EC), receiver_global.reshape(tiles, EC), levels.reshape(tiles, EC), valid.reshape(tiles, EC))
    aggregated, edge_new = lax.scan(tile_step, jnp.zeros((NODES, D), jnp.float32), items)
    edges_out = edge_new.reshape(N_ROW, N_COL, EC, D)
    node_pre = jnp.dot(nodes, node_w1[0], preferred_element_type=jnp.float32)
    node_pre = node_pre + jnp.dot(aggregated.astype(jnp.bfloat16), node_w1[1], preferred_element_type=jnp.float32)
    nodes_out = (nodes.astype(jnp.float32) + mlp_tail(node_pre, node_w2, node_gain)).astype(jnp.bfloat16)
    source_ids = jnp.arange(tiles, dtype=jnp.int32)[None, :, None] * block + jnp.transpose(send_rows, (1, 0, 2))
    buffer_global = source_ids.reshape(tiles, tiles * RQ)
    band = jnp.arange(GRID, dtype=jnp.int32) // GC
    cell_senders = buffer_global[band[:, None], dec_index]
    node_dec = jnp.dot(nodes_out, dec_w1[1], preferred_element_type=jnp.float32)
    grid_part = jnp.dot(grid, dec_w1[0], preferred_element_type=jnp.float32)
    dec_pre = grid_part[:, None, :] + node_dec[cell_senders]
    messages = mlp_tail(dec_pre.reshape(GRID * KD, D), dec_w2, dec_gain).reshape(GRID, KD, D)
    grid_out = (grid.astype(jnp.float32) + lax.optimization_barrier(jnp.sum(messages, axis=1))).astype(jnp.bfloat16)
    return (nodes_out, edges_out, grid_out)
```

```python
import functools

import jax
import jax.numpy as jnp
from jax import lax
from jax.experimental import pallas as pl
from jax.experimental.pallas import tpu as pltpu
from jax.sharding import PartitionSpec as P

EPSILON = 1e-05
LANES = 128
EDGE_ROWS = 512
CELL_ROWS = 256
VMEM_BYTES = 56 * 1024 * 1024


def dot(a, b):
    return jnp.dot(a, b, preferred_element_type=jnp.float32)


def silu_low(pre):
    half = 0.5 * pre
    return (half + half * jnp.tanh(half)).astype(jnp.bfloat16)


def center_scale(values):
    center = values - jnp.mean(values, axis=-1, keepdims=True)
    spread = jnp.mean(center * center, axis=-1, keepdims=True)
    return center, lax.rsqrt(spread + EPSILON)


def column_hot(ids, count):
    lanes = lax.broadcasted_iota(jnp.int32, (ids.shape[0], count), 1)
    return (ids == lanes).astype(jnp.bfloat16)


def row_hot(ids, count):
    rows = lax.broadcasted_iota(jnp.int32, (count, ids.shape[1]), 0)
    return (ids == rows).astype(jnp.bfloat16)


def project_kernel(nodes_ref, weight_ref, send_ref, recv_ref):
    nodes = nodes_ref[...]
    send = dot(nodes, weight_ref[1]).astype(jnp.bfloat16)
    recv = dot(nodes, weight_ref[2]).astype(jnp.bfloat16)
    for k in range(send_ref.shape[0]):
        send_ref[k] = send
    for k in range(recv_ref.shape[0]):
        recv_ref[k] = recv


def edge_kernel(
    count_ref,
    ids_ref,
    rows_ref,
    send_ref,
    recv_ref,
    w1_ref,
    bias_ref,
    w2_ref,
    gain_ref,
    out_ref,
    sum_ref,
    total,
):
    step = pl.program_id(0)
    rows = rows_ref.shape[0]
    parts = rows // LANES
    count = count_ref[0, 0]

    @pl.when(step == 0)
    def _():
        total[...] = jnp.zeros_like(total)

    @pl.when(step * rows >= count)
    def _():
        out_ref[...] = rows_ref[...]

    @pl.when(step * rows < count)
    def _():
        ids = ids_ref[0]
        columns = jnp.transpose(ids)

        def gather_hot(kind, size):
            return jnp.concatenate(
                [
                    column_hot(columns[:, kind * parts + p : kind * parts + p + 1], size)
                    for p in range(parts)
                ],
                axis=0,
            )

        edge_rows = rows_ref[...]
        pre = dot(edge_rows, w1_ref[0])
        pre = pre + dot(gather_hot(0, send_ref.shape[0]), send_ref[...])
        pre = pre + dot(gather_hot(1, recv_ref.shape[0]), recv_ref[...])
        pre = pre + dot(gather_hot(2, bias_ref.shape[0]), bias_ref[...])
        center, scale = center_scale(dot(silu_low(pre), w2_ref[...]))
        slot = step * rows + lax.broadcasted_iota(jnp.int32, (rows, 1), 0)
        scale = jnp.where(slot < count, scale, 0.0)
        message = (center * scale * gain_ref[...]).astype(jnp.bfloat16)
        out_ref[...] = (edge_rows.astype(jnp.float32) + message.astype(jnp.float32)).astype(
            jnp.bfloat16
        )
        spread_hot = jnp.concatenate(
            [
                row_hot(ids[parts + p : parts + p + 1, :], recv_ref.shape[0])
                for p in range(parts)
            ],
            axis=1,
        )
        total[...] += dot(spread_hot, message)

    @pl.when(step == pl.num_programs(0) - 1)
    def _():
        sum_ref[...] = total[...].astype(jnp.bfloat16)


def node_kernel(
    parts_ref, nodes_ref, w1_ref, w2_ref, gain_ref, dec_w1_ref, picks_ref, out_ref, picked_ref
):
    low = jnp.sum(parts_ref[...].astype(jnp.float32), axis=0).astype(jnp.bfloat16)
    nodes = nodes_ref[...]
    pre = dot(nodes, w1_ref[0]) + dot(low, w1_ref[1])
    center, scale = center_scale(dot(silu_low(pre), w2_ref[...]))
    fresh = (nodes.astype(jnp.float32) + center * scale * gain_ref[...]).astype(jnp.bfloat16)
    out_ref[...] = fresh
    projected = dot(fresh, dec_w1_ref[1]).astype(jnp.bfloat16)
    columns = jnp.transpose(picks_ref[...])
    for p in range(picks_ref.shape[0]):
        hot = column_hot(columns[:, p : p + 1], nodes.shape[0])
        picked_ref[p * LANES : (p + 1) * LANES, :] = dot(hot, projected).astype(jnp.bfloat16)


def decode_kernel(ids_ref, grid_ref, table_ref, w1_ref, w2_ref, gain_ref, out_ref):
    cells = grid_ref.shape[0]
    parts = cells // LANES
    fan = ids_ref.shape[1] // parts
    grid = grid_ref[...]
    shared = dot(grid, w1_ref[0])
    columns = jnp.transpose(ids_ref[0])
    message = jnp.zeros(grid.shape, jnp.float32)
    for e in range(fan):
        hot = jnp.concatenate(
            [
                column_hot(columns[:, e * parts + p : e * parts + p + 1], table_ref.shape[0])
                for p in range(parts)
            ],
            axis=0,
        )
        pre = shared + dot(hot, table_ref[...])
        center, scale = center_scale(dot(silu_low(pre), w2_ref[...]))
        message = message + center * scale
    out_ref[...] = (grid.astype(jnp.float32) + message * gain_ref[...]).astype(jnp.bfloat16)


def whole(array):
    return pl.BlockSpec(array.shape, lambda *_: (0,) * array.ndim, pipeline_mode=pl.Buffered(1))


def params():
    return pltpu.CompilerParams(vmem_limit_bytes=VMEM_BYTES)


def on_device(
    nodes,
    edges,
    senders,
    receivers,
    levels,
    counts,
    edge_w1,
    level_bias,
    edge_w2,
    edge_gain,
    node_w1,
    node_w2,
    node_gain,
    grid,
    send_rows,
    dec_index,
    dec_w1,
    dec_w2,
    dec_gain,
):
    bf16, f32 = jnp.bfloat16, jnp.float32
    block, width = nodes.shape
    row_size, col_size = lax.axis_size("row"), lax.axis_size("col")
    slots = edges.shape[2]
    peers, per_peer = send_rows.shape[1:]
    cells, fan = dec_index.shape

    send_copies, recv_copies = pl.pallas_call(
        project_kernel,
        out_shape=(
            jax.ShapeDtypeStruct((row_size, block, width), bf16),
            jax.ShapeDtypeStruct((col_size, block, width), bf16),
        ),
        compiler_params=params(),
    )(nodes, edge_w1)
    send_table = lax.all_to_all(send_copies, "row", 0, 0, tiled=True).reshape(-1, width)
    recv_table = lax.all_to_all(recv_copies, "col", 0, 0, tiled=True).reshape(-1, width)

    steps = slots // EDGE_ROWS
    edge_ids = jnp.concatenate(
        [
            ids.reshape(steps, EDGE_ROWS // LANES, LANES)
            for ids in (senders, receivers, levels)
        ],
        axis=1,
    )
    edge_ids = jnp.pad(edge_ids, ((0, 0), (0, -edge_ids.shape[1] % 8), (0, 0)))
    bias = jnp.pad(level_bias, ((0, -level_bias.shape[0] % 16), (0, 0)))
    gain = edge_gain.reshape(1, width)
    edges_out, partial_sum = pl.pallas_call(
        edge_kernel,
        grid_spec=pltpu.PrefetchScalarGridSpec(
            num_scalar_prefetch=1,
            grid=(steps,),
            in_specs=[
                pl.BlockSpec((1,) + edge_ids.shape[1:], lambda i, _: (i, 0, 0)),
                pl.BlockSpec((EDGE_ROWS, width), lambda i, _: (i, 0)),
                whole(send_table),
                whole(recv_table),
                pl.BlockSpec((1, width, width), lambda *_: (0, 0, 0), pipeline_mode=pl.Buffered(1)),
                whole(bias),
                whole(edge_w2),
                whole(gain),
            ],
            out_specs=(
                pl.BlockSpec((EDGE_ROWS, width), lambda i, _: (i, 0)),
                pl.BlockSpec(recv_table.shape, lambda *_: (0, 0)),
            ),
            scratch_shapes=[pltpu.VMEM(recv_table.shape, f32)],
        ),
        out_shape=(
            jax.ShapeDtypeStruct((slots, width), bf16),
            jax.ShapeDtypeStruct(recv_table.shape, bf16),
        ),
        compiler_params=params(),
    )(
        counts,
        edge_ids,
        edges.reshape(slots, width),
        send_table,
        recv_table,
        edge_w1,
        bias,
        edge_w2,
        gain,
    )

    node_parts = lax.all_to_all(
        partial_sum.reshape(col_size, block, width), "col", 0, 0, tiled=True
    )
    nodes_out, picked = pl.pallas_call(
        node_kernel,
        out_shape=(
            jax.ShapeDtypeStruct((block, width), bf16),
            jax.ShapeDtypeStruct((peers * per_peer, width), bf16),
        ),
        compiler_params=params(),
    )(
        node_parts,
        nodes,
        node_w1,
        node_w2,
        node_gain.reshape(1, width),
        dec_w1,
        send_rows.reshape(-1, LANES),
    )

    table = lax.all_to_all(
        picked.reshape(peers, per_peer, width), ("row", "col"), 0, 0, tiled=True
    ).reshape(-1, width)
    dec_steps = cells // CELL_ROWS
    dec_parts = CELL_ROWS // LANES
    dec_ids = (
        dec_index.T.reshape(fan, dec_steps, dec_parts, LANES)
        .transpose(1, 0, 2, 3)
        .reshape(dec_steps, fan * dec_parts, LANES)
    )
    dec_scale = dec_gain.reshape(1, width)
    grid_out = pl.pallas_call(
        decode_kernel,
        grid=(dec_steps,),
        in_specs=[
            pl.BlockSpec((1,) + dec_ids.shape[1:], lambda i: (i, 0, 0)),
            pl.BlockSpec((CELL_ROWS, width), lambda i: (i, 0)),
            whole(table),
            pl.BlockSpec((1, width, width), lambda *_: (0, 0, 0), pipeline_mode=pl.Buffered(1)),
            whole(dec_w2),
            whole(dec_scale),
        ],
        out_specs=pl.BlockSpec((CELL_ROWS, width), lambda i: (i, 0)),
        out_shape=jax.ShapeDtypeStruct((cells, width), bf16),
        compiler_params=params(),
    )(dec_ids, grid, table, dec_w1, dec_w2, dec_scale)
    return (nodes_out, edges_out.reshape(edges.shape), grid_out)


def solution(mesh):
    tile = P("row", "col", None)
    split = P(("row", "col"), None)
    return jax.shard_map(
        on_device,
        mesh=mesh,
        in_specs=(
            split,
            P("row", "col", None, None),
            tile,
            tile,
            tile,
            P("row", "col"),
            P(),
            P(),
            P(),
            P(),
            P(),
            P(),
            P(),
            split,
            P(("row", "col"), None, None),
            split,
            P(),
            P(),
            P(),
        ),
        out_specs=(split, P("row", "col", None, None), split),
        check_vma=False,
    )
```

```python
import jax
import jax.numpy as jnp
from jax import lax
from jax.experimental import pallas as pl
from jax.experimental.pallas import tpu as pltpu
from jax.sharding import PartitionSpec as P

EPSILON = 1e-05
LANES = 128
EDGE_ROWS = 1024
CHUNK = 256
CELL_ROWS = 256


def dot(a, b):
    return jnp.dot(a, b, preferred_element_type=jnp.float32)


def silu_half(half):
    return (half + half * jnp.tanh(half)).astype(jnp.bfloat16)


def center_scale(values):
    center = values - jnp.mean(values, axis=-1, keepdims=True)
    spread = jnp.mean(center * center, axis=-1, keepdims=True)
    return center, lax.rsqrt(spread + EPSILON)


def column_hot(ids, count):
    lanes = lax.broadcasted_iota(jnp.int32, (ids.shape[0], count), 1)
    return (ids == lanes).astype(jnp.bfloat16)


def stacked_hot(columns, first, number, count):
    return jnp.concatenate(
        [column_hot(columns[:, p : p + 1], count) for p in range(first, first + number)], axis=0
    )


def row_hot(ids, count):
    rows = lax.broadcasted_iota(jnp.int32, (count, ids.shape[1]), 0)
    return (ids == rows).astype(jnp.bfloat16)


def project_kernel(nodes_ref, send_weight_ref, recv_weight_ref, send_ref, recv_ref):
    nodes = nodes_ref[...]
    recv = (0.5 * dot(nodes, recv_weight_ref[0])).astype(jnp.bfloat16)
    for k in range(recv_ref.shape[0]):
        recv_ref[k] = recv
    send_ref[...] = (0.5 * dot(nodes, send_weight_ref[0])).astype(jnp.bfloat16)


def edge_first_kernel(ids_ref, rows_ref, w1_ref, bias_ref, half_ref):
    columns = jnp.transpose(ids_ref[0])
    levels = bias_ref.shape[0]
    for p in range(rows_ref.shape[0] // CHUNK):
        part = slice(p * CHUNK, (p + 1) * CHUNK)
        hot = stacked_hot(columns, p * CHUNK // LANES, CHUNK // LANES, levels)
        half_ref[part, :] = 0.5 * (dot(rows_ref[part, :], w1_ref[0]) + dot(hot, bias_ref[...]))


def grid_first_kernel(grid_ref, w1_ref, half_ref):
    half_ref[...] = 0.5 * dot(grid_ref[...], w1_ref[0])


def edge_kernel(
    place_ref,
    ids_ref,
    rows_ref,
    half_ref,
    near_ref,
    far1_ref,
    far2_ref,
    far3_ref,
    recv_ref,
    w2_ref,
    gain_ref,
    out_ref,
    sum_ref,
    total,
    table,
    messages,
):
    step = pl.program_id(0)
    rows = rows_ref.shape[0]
    parts = rows // LANES
    count, chip = place_ref[0], place_ref[1]
    send_count = table.shape[0] - recv_ref.shape[0]

    @pl.when(step == 0)
    def _():
        total[...] = jnp.zeros_like(total)
        sources = (near_ref, far1_ref, far2_ref, far3_ref)
        span = near_ref.shape[0]
        for k, source in enumerate(sources):
            owner = lax.rem(chip - k + len(sources), len(sources))
            table[pl.ds(pl.multiple_of(owner * span, span), span), :] = source[...]
        table[send_count:, :] = recv_ref[...]

    @pl.when(step * rows >= count)
    def _():
        out_ref[...] = rows_ref[...]

    @pl.when(step * rows < count)
    def _():
        ids = ids_ref[0]
        columns = jnp.transpose(ids)

        def first(c):
            hot = jnp.concatenate(
                [
                    stacked_hot(columns, c * CHUNK // LANES, CHUNK // LANES, send_count),
                    stacked_hot(
                        columns, parts + c * CHUNK // LANES, CHUNK // LANES, recv_ref.shape[0]
                    ),
                ],
                axis=1,
            )
            return silu_half(half_ref[c * CHUNK : (c + 1) * CHUNK, :] + dot(hot, table[...]))

        def second(c, hidden):
            part = slice(c * CHUNK, (c + 1) * CHUNK)
            center, scale = center_scale(dot(hidden, w2_ref[...]))
            slot = step * rows + c * CHUNK + lax.broadcasted_iota(jnp.int32, (CHUNK, 1), 0)
            scale = jnp.where(slot < count, scale, 0.0)
            message = (center * scale * gain_ref[...]).astype(jnp.bfloat16)
            out_ref[part, :] = (
                rows_ref[part, :].astype(jnp.float32) + message.astype(jnp.float32)
            ).astype(jnp.bfloat16)
            messages[part, :] = message

        hidden = first(0)
        for c in range(rows // CHUNK):
            later = first(c + 1) if (c + 1) * CHUNK < rows else None
            second(c, hidden)
            hidden = later
        spread_hot = jnp.concatenate(
            [
                row_hot(ids[parts + p : parts + p + 1, :], recv_ref.shape[0])
                for p in range(parts)
            ],
            axis=1,
        )
        total[...] += dot(spread_hot, messages[...])

    @pl.when(step == pl.num_programs(0) - 1)
    def _():
        sum_ref[...] = total[...].astype(jnp.bfloat16)


def node_kernel(
    parts_ref, nodes_ref, w1_ref, w2_ref, gain_ref, dec_w1_ref, picks_ref, out_ref, picked_ref, wide
):
    low = jnp.sum(parts_ref[...].astype(jnp.float32), axis=0).astype(jnp.bfloat16)
    nodes = nodes_ref[...]
    pre = dot(nodes, w1_ref[0]) + dot(low, w1_ref[1])
    center, scale = center_scale(dot(silu_half(0.5 * pre), w2_ref[...]))
    fresh = (nodes.astype(jnp.float32) + center * scale * gain_ref[...]).astype(jnp.bfloat16)
    out_ref[...] = fresh
    projected = (0.5 * dot(fresh, dec_w1_ref[0])).astype(jnp.bfloat16)
    peers, strips, _ = picked_ref.shape
    columns = jnp.transpose(picks_ref[...])
    groups = strips // picks_ref.shape[0]
    for j in range(picks_ref.shape[0]):
        chosen = dot(column_hot(columns[:, j : j + 1], nodes.shape[0]), projected)
        for q in range(groups):
            wide[pl.ds(j * groups + q, peers, stride=strips), :] = chosen[
                :, q * LANES : (q + 1) * LANES
            ]
    picked_ref[...] = wide[...].reshape(picked_ref.shape).astype(jnp.bfloat16)


def decode_kernel(
    ids_ref, grid_ref, half_ref, received_ref, w2_ref, gain_ref, out_ref, wide, table
):
    cells = grid_ref.shape[0]
    parts = cells // LANES
    fan = ids_ref.shape[1] // parts
    peers, strips, _ = received_ref.shape
    groups = table.shape[1] // LANES
    per_peer = strips // groups

    @pl.when(pl.program_id(0) == 0)
    def _():
        wide[...] = received_ref[...].astype(jnp.float32).reshape(wide.shape)
        for j in range(per_peer):
            for q in range(groups):
                table[j * peers : (j + 1) * peers, q * LANES : (q + 1) * LANES] = wide[
                    pl.ds(j * groups + q, peers, stride=strips), :
                ].astype(jnp.bfloat16)

    ids = ids_ref[0]
    columns = jnp.transpose(lax.rem(ids, per_peer) * peers + lax.div(ids, per_peer))
    shared = half_ref[...]

    def first(e):
        hot = stacked_hot(columns, e * parts, parts, table.shape[0])
        return silu_half(shared + dot(hot, table[...]))

    message = jnp.zeros(grid_ref.shape, jnp.float32)
    hidden = first(0)
    for e in range(fan):
        later = first(e + 1) if e + 1 < fan else None
        center, scale = center_scale(dot(hidden, w2_ref[...]))
        message = message + center * scale
        hidden = later
    out_ref[...] = (grid_ref[...].astype(jnp.float32) + message * gain_ref[...]).astype(
        jnp.bfloat16
    )


def whole(array):
    return pl.BlockSpec(array.shape, lambda *_: (0,) * array.ndim, pipeline_mode=pl.Buffered(1))


def layer(k, width):
    return pl.BlockSpec((1, width, width), lambda *_: (k, 0, 0), pipeline_mode=pl.Buffered(1))


def params(mib):
    return pltpu.CompilerParams(vmem_limit_bytes=mib * 1024 * 1024)


def on_device(
    nodes,
    edges,
    senders,
    receivers,
    levels,
    counts,
    edge_w1,
    level_bias,
    edge_w2,
    edge_gain,
    node_w1,
    node_w2,
    node_gain,
    grid,
    send_rows,
    dec_index,
    dec_w1,
    dec_w2,
    dec_gain,
):
    bf16, f32 = jnp.bfloat16, jnp.float32
    block, width = nodes.shape
    row_size, col_size = lax.axis_size("row"), lax.axis_size("col")
    slots = edges.shape[2]
    peers, per_peer = send_rows.shape[1:]
    cells, fan = dec_index.shape
    recv_count = block * col_size
    rows = edges.reshape(slots, width)

    send_own, recv_copies = pl.pallas_call(
        project_kernel,
        grid=(1,),
        in_specs=[whole(nodes), layer(1, width), layer(2, width)],
        out_specs=(
            pl.BlockSpec((block, width), lambda i: (0, 0)),
            pl.BlockSpec((col_size, block, width), lambda i: (0, 0, 0)),
        ),
        out_shape=(
            jax.ShapeDtypeStruct((block, width), bf16),
            jax.ShapeDtypeStruct((col_size, block, width), bf16),
        ),
        compiler_params=params(57),
        name="project",
    )(nodes, edge_w1, edge_w1)
    recv_table = lax.all_to_all(recv_copies, "col", 0, 0, tiled=True).reshape(-1, width)
    own = lax.axis_index("row")
    send_pair = lax.ppermute(send_own, "row", [(i, i ^ 1) for i in range(row_size)])
    near = jnp.where(
        own % 2 == 0,
        jnp.concatenate([send_own, send_pair]),
        jnp.concatenate([send_pair, send_own]),
    )
    rows_first, grid_rows, near = lax.optimization_barrier((rows, grid, near))
    far = [
        lax.ppermute(near, "row", [(i, (i + 2 * k) % row_size) for i in range(row_size)])
        for k in range(1, row_size // 2)
    ]
    steps = slots // EDGE_ROWS
    parts = EDGE_ROWS // LANES
    level_ids = levels.reshape(steps, parts, LANES)
    edge_half = pl.pallas_call(
        edge_first_kernel,
        grid=(steps,),
        in_specs=[
            pl.BlockSpec((1, parts, LANES), lambda i: (i, 0, 0)),
            pl.BlockSpec((EDGE_ROWS, width), lambda i: (i, 0)),
            layer(0, width),
            whole(level_bias),
        ],
        out_specs=pl.BlockSpec((EDGE_ROWS, width), lambda i: (i, 0)),
        out_shape=jax.ShapeDtypeStruct((slots, width), f32),
        compiler_params=params(57),
        cost_estimate=pl.CostEstimate(
            flops=2 * slots * width * width, bytes_accessed=6 * slots * width, transcendentals=0
        ),
        name="edge_first",
    )(level_ids, rows_first, edge_w1, level_bias)
    grid_half = pl.pallas_call(
        grid_first_kernel,
        grid=(cells // CELL_ROWS,),
        in_specs=[pl.BlockSpec((CELL_ROWS, width), lambda i: (i, 0)), layer(0, width)],
        out_specs=pl.BlockSpec((CELL_ROWS, width), lambda i: (i, 0)),
        out_shape=jax.ShapeDtypeStruct((cells, width), f32),
        compiler_params=params(57),
        cost_estimate=pl.CostEstimate(
            flops=2 * cells * width * width, bytes_accessed=6 * cells * width, transcendentals=0
        ),
        name="grid_first",
    )(grid_rows, dec_w1)

    edge_ids = jnp.concatenate(
        [ids.reshape(steps, parts, LANES) for ids in (senders, receivers)], axis=1
    )
    place = jnp.stack([counts[0, 0], own // 2])
    gain = edge_gain.reshape(1, width)
    block_spec = pl.BlockSpec((EDGE_ROWS, width), lambda i, _: (i, 0))
    edges_out, partial_sum = pl.pallas_call(
        edge_kernel,
        grid_spec=pltpu.PrefetchScalarGridSpec(
            num_scalar_prefetch=1,
            grid=(steps,),
            in_specs=[
                pl.BlockSpec((1, 2 * parts, LANES), lambda i, _: (i, 0, 0)),
                block_spec,
                block_spec,
                whole(near),
                *(whole(rows_far) for rows_far in far),
                whole(recv_table),
                whole(edge_w2),
                whole(gain),
            ],
            out_specs=(block_spec, pl.BlockSpec((recv_count, width), lambda *_: (0, 0))),
            scratch_shapes=[
                pltpu.VMEM((recv_count, width), f32),
                pltpu.VMEM((block * row_size + recv_count, width), bf16),
                pltpu.VMEM((EDGE_ROWS, width), bf16),
            ],
        ),
        out_shape=(
            jax.ShapeDtypeStruct((slots, width), bf16),
            jax.ShapeDtypeStruct((recv_count, width), bf16),
        ),
        compiler_params=params(50),
        name="edges",
    )(place, edge_ids, rows, edge_half, near, *far, recv_table, edge_w2, gain)

    node_parts = lax.all_to_all(
        partial_sum.reshape(col_size, block, width), "col", 0, 0, tiled=True
    )
    strips = per_peer * width // LANES
    picks = send_rows[0].T
    node_scale = node_gain.reshape(1, width)
    nodes_out, picked = pl.pallas_call(
        node_kernel,
        grid=(1,),
        in_specs=[
            whole(node_parts),
            whole(nodes),
            whole(node_w1),
            whole(node_w2),
            whole(node_scale),
            layer(1, width),
            whole(picks),
        ],
        out_specs=(
            pl.BlockSpec((block, width), lambda i: (0, 0)),
            pl.BlockSpec((peers, strips, LANES), lambda i: (0, 0, 0)),
        ),
        out_shape=(
            jax.ShapeDtypeStruct((block, width), bf16),
            jax.ShapeDtypeStruct((peers, strips, LANES), bf16),
        ),
        scratch_shapes=[pltpu.VMEM((peers * strips, LANES), f32)],
        compiler_params=params(12),
        name="nodes",
    )(node_parts, nodes, node_w1, node_w2, node_scale, dec_w1, picks)

    received = lax.all_to_all(picked, ("row", "col"), 0, 0, tiled=True)
    dec_steps = cells // CELL_ROWS
    dec_parts = CELL_ROWS // LANES
    dec_ids = (
        dec_index.T.reshape(fan, dec_steps, dec_parts, LANES)
        .transpose(1, 0, 2, 3)
        .reshape(dec_steps, fan * dec_parts, LANES)
    )
    dec_scale = dec_gain.reshape(1, width)
    cell_spec = pl.BlockSpec((CELL_ROWS, width), lambda i: (i, 0))
    grid_out = pl.pallas_call(
        decode_kernel,
        grid=(dec_steps,),
        in_specs=[
            pl.BlockSpec((1, fan * dec_parts, LANES), lambda i: (i, 0, 0)),
            cell_spec,
            cell_spec,
            whole(received),
            whole(dec_w2),
            whole(dec_scale),
        ],
        out_specs=cell_spec,
        out_shape=jax.ShapeDtypeStruct((cells, width), bf16),
        scratch_shapes=[
            pltpu.VMEM((peers * strips, LANES), f32),
            pltpu.VMEM((peers * per_peer, width), bf16),
        ],
        compiler_params=params(52),
        name="decoder",
    )(dec_ids, grid, grid_half, received, dec_w2, dec_scale)
    return (nodes_out, edges_out.reshape(edges.shape), grid_out)


def solution(mesh):
    tile = P("row", "col", None)
    split = P(("row", "col"), None)
    return jax.shard_map(
        on_device,
        mesh=mesh,
        in_specs=(
            split,
            P("row", "col", None, None),
            tile,
            tile,
            tile,
            P("row", "col"),
            P(),
            P(),
            P(),
            P(),
            P(),
            P(),
            P(),
            split,
            P(("row", "col"), None, None),
            split,
            P(),
            P(),
            P(),
        ),
        out_specs=(split, P("row", "col", None, None), split),
        check_vma=False,
    )
```

```python
import jax
import jax.numpy as jnp
from jax import lax
from jax.experimental import pallas as pl
from jax.experimental.pallas import tpu as pltpu
from jax.sharding import PartitionSpec as P

EPSILON = 1e-05
LANES = 128
EDGE_ROWS = 1024
CHUNK = 256
AHEAD = 2


def dot(a, b):
    return jnp.dot(a, b, preferred_element_type=jnp.float32)


def silu_half(half):
    return (half + half * jnp.tanh(half)).astype(jnp.bfloat16)


def center_scale(values):
    center = values - jnp.mean(values, axis=-1, keepdims=True)
    spread = jnp.mean(center * center, axis=-1, keepdims=True)
    return center, lax.rsqrt(spread + EPSILON)


def column_hot(ids, count):
    lanes = lax.broadcasted_iota(jnp.int32, (ids.shape[0], count), 1)
    return (ids == lanes).astype(jnp.bfloat16)


def stacked_hot(columns, first, number, count):
    return jnp.concatenate(
        [column_hot(columns[:, p : p + 1], count) for p in range(first, first + number)], axis=0
    )


def row_hot(ids, count):
    rows = lax.broadcasted_iota(jnp.int32, (count, ids.shape[1]), 0)
    return (ids == rows).astype(jnp.bfloat16)


def project_kernel(nodes_ref, send_weight_ref, recv_weight_ref, send_ref, recv_ref):
    nodes = nodes_ref[...]
    recv = (0.5 * dot(nodes, recv_weight_ref[0])).astype(jnp.bfloat16)
    for k in range(recv_ref.shape[0]):
        recv_ref[k] = recv
    send_ref[...] = (0.5 * dot(nodes, send_weight_ref[0])).astype(jnp.bfloat16)


def edge_first_kernel(
    ids_ref, rows_ref, w1_ref, bias_ref, half_ref, rows, half, weight, row_sems, half_sems, weight_sem
):
    blocks = ids_ref.shape[0]
    span = ids_ref.shape[1] * LANES
    weight_copy = pltpu.make_async_copy(w1_ref.at[0], weight, weight_sem)
    weight_copy.start()
    copies = [
        pltpu.make_async_copy(
            rows_ref.at[pl.ds(k * span, span)], rows.at[pl.ds(k * span, span)], row_sems.at[k]
        )
        for k in range(blocks)
    ]
    for copy in copies[:AHEAD]:
        copy.start()
    weight_copy.wait()
    outs = []
    for k in range(blocks):
        columns = jnp.transpose(ids_ref[k])
        hot = stacked_hot(columns, 0, ids_ref.shape[1], bias_ref.shape[0])
        copies[k].wait()
        if k + AHEAD < blocks:
            copies[k + AHEAD].start()
        part = slice(k * span, (k + 1) * span)
        product = dot(rows[part, :], weight[...]) + dot(hot, bias_ref[...])
        half[part, :] = (0.5 * product).astype(jnp.bfloat16)
        place = pl.ds(k * span, span)
        outs.append(pltpu.make_async_copy(half.at[place], half_ref.at[place], half_sems.at[k]))
        outs[-1].start()
    for out in outs:
        out.wait()


def edge_kernel(
    place_ref,
    ids_ref,
    rows_ref,
    half_ref,
    near_ref,
    far1_ref,
    far2_ref,
    far3_ref,
    recv_ref,
    w2_ref,
    gain_ref,
    out_ref,
    sum_ref,
    total,
    table,
    messages,
    edge_rows,
    half,
    row_sems,
    half_sems,
    out_sems,
):
    blocks = ids_ref.shape[0]
    parts = ids_ref.shape[1] // 2
    rows = parts * LANES
    count, chip = place_ref[0], place_ref[1]
    send_count = table.shape[0] - recv_ref.shape[0]

    def stream(source, target, sems, k):
        place = pl.ds(pl.multiple_of(k * rows, rows), rows)
        return pltpu.make_async_copy(source.at[place], target.at[place], sems.at[k])

    for k in range(blocks):
        stream(half_ref, half, half_sems, k).start()
        stream(rows_ref, edge_rows, row_sems, k).start()
    total[...] = jnp.zeros_like(total)
    sources = (near_ref, far1_ref, far2_ref, far3_ref)
    span = near_ref.shape[0]
    for k, source in enumerate(sources):
        owner = lax.rem(chip - k + len(sources), len(sources))
        table[pl.ds(pl.multiple_of(owner * span, span), span), :] = source[...]
    table[send_count:, :] = recv_ref[...]

    @pl.loop(0, blocks)
    def _(step):
        base = pl.multiple_of(step * rows, rows)

        stream(half_ref, half, half_sems, step).wait()
        stream(rows_ref, edge_rows, row_sems, step).wait()

        @pl.when(base >= count)
        def _():
            stream(edge_rows, out_ref, out_sems, step).start()

        @pl.when(base < count)
        def _():
            ids = ids_ref[step]
            columns = jnp.transpose(ids)

            def first(c):
                hot = jnp.concatenate(
                    [
                        stacked_hot(columns, c * CHUNK // LANES, CHUNK // LANES, send_count),
                        stacked_hot(
                            columns, parts + c * CHUNK // LANES, CHUNK // LANES, recv_ref.shape[0]
                        ),
                    ],
                    axis=1,
                )
                known = half[pl.ds(base + c * CHUNK, CHUNK), :].astype(jnp.float32)
                return silu_half(known + dot(hot, table[...]))

            def second(c, hidden):
                center, scale = center_scale(dot(hidden, w2_ref[...]))
                slot = base + c * CHUNK + lax.broadcasted_iota(jnp.int32, (CHUNK, 1), 0)
                scale = jnp.where(slot < count, scale, 0.0)
                message = (center * scale * gain_ref[...]).astype(jnp.bfloat16)
                messages[c * CHUNK : (c + 1) * CHUNK, :] = message
                place = pl.ds(base + c * CHUNK, CHUNK)
                edge_rows[place, :] = (
                    edge_rows[place, :].astype(jnp.float32) + message.astype(jnp.float32)
                ).astype(jnp.bfloat16)

            hidden = first(0)
            for c in range(rows // CHUNK):
                later = first(c + 1) if (c + 1) * CHUNK < rows else None
                second(c, hidden)
                hidden = later
            stream(edge_rows, out_ref, out_sems, step).start()
            spread_hot = jnp.concatenate(
                [
                    row_hot(ids[parts + p : parts + p + 1, :], recv_ref.shape[0])
                    for p in range(parts)
                ],
                axis=1,
            )
            total[...] += dot(spread_hot, messages[...])

    sum_ref[...] = total[...].astype(jnp.bfloat16)
    for k in range(blocks):
        stream(edge_rows, out_ref, out_sems, k).wait()


def grid_first_kernel(ids_ref, grid_ref, w1_ref, half_ref, hot_ref):
    cells = grid_ref.shape[0]
    half_ref[...] = (0.5 * dot(grid_ref[...], w1_ref[0])).astype(jnp.bfloat16)
    per_peer = hot_ref.shape[1] // LANES
    ids = ids_ref[...]
    columns = jnp.transpose(lax.rem(ids, per_peer) * LANES + lax.div(ids, per_peer))
    parts = CHUNK // LANES
    fan = hot_ref.shape[0] // cells
    for b in range(cells // CHUNK):
        for e in range(fan):
            start = (b * fan + e) * CHUNK
            hot_ref[start : start + CHUNK, :] = stacked_hot(
                columns, e * (cells // LANES) + b * parts, parts, hot_ref.shape[1]
            )


def node_kernel(
    parts_ref, nodes_ref, w1_ref, w2_ref, gain_ref, dec_w1_ref, picks_ref, out_ref, picked_ref, wide
):
    low = jnp.sum(parts_ref[...].astype(jnp.float32), axis=0).astype(jnp.bfloat16)
    nodes = nodes_ref[...]
    pre = dot(nodes, w1_ref[0]) + dot(low, w1_ref[1])
    center, scale = center_scale(dot(silu_half(0.5 * pre), w2_ref[...]))
    fresh = (nodes.astype(jnp.float32) + center * scale * gain_ref[...]).astype(jnp.bfloat16)
    out_ref[...] = fresh
    projected = (0.5 * dot(fresh, dec_w1_ref[0])).astype(jnp.bfloat16)
    peers, strips, _ = picked_ref.shape
    columns = jnp.transpose(picks_ref[...])
    groups = strips // picks_ref.shape[0]
    for j in range(picks_ref.shape[0]):
        chosen = dot(column_hot(columns[:, j : j + 1], nodes.shape[0]), projected)
        for q in range(groups):
            wide[pl.ds(j * groups + q, peers, stride=strips), :] = chosen[
                :, q * LANES : (q + 1) * LANES
            ]
    picked_ref[...] = wide[...].reshape(picked_ref.shape).astype(jnp.bfloat16)


def decode_kernel(
    hot_ref,
    grid_ref,
    half_ref,
    received_ref,
    w2_ref,
    gain_ref,
    out_ref,
    received,
    w2,
    hot,
    half,
    grid,
    wide,
    table,
    result,
    sems,
    hot_sems,
    half_sems,
    out_sems,
):
    cells = grid_ref.shape[0]
    blocks = cells // CHUNK
    fan = hot_ref.shape[0] // cells
    peers, strips, _ = received_ref.shape
    groups = table.shape[1] // LANES

    def stream(source, target, sems, k, rows):
        place = pl.ds(k * rows, rows)
        return pltpu.make_async_copy(source.at[place], target.at[place], sems.at[k])

    received_copy = pltpu.make_async_copy(received_ref, received, sems.at[0])
    w2_copy = pltpu.make_async_copy(w2_ref, w2, sems.at[1])
    grid_copy = pltpu.make_async_copy(grid_ref, grid, sems.at[2])
    def fetch(b):
        stream(hot_ref, hot, hot_sems, b, fan * CHUNK).start()
        stream(half_ref, half, half_sems, b, CHUNK).start()

    received_copy.start()
    fetch(0)
    w2_copy.start()
    received_copy.wait()
    wide[...] = received[...].astype(jnp.float32).reshape(wide.shape)
    for j in range(strips // groups):
        for q in range(groups):
            table[j * peers : (j + 1) * peers, q * LANES : (q + 1) * LANES] = wide[
                pl.ds(j * groups + q, peers, stride=strips), :
            ].astype(jnp.bfloat16)

    def first(b, e):
        if e == 0:
            stream(hot_ref, hot, hot_sems, b, fan * CHUNK).wait()
            stream(half_ref, half, half_sems, b, CHUNK).wait()
            if b == 0:
                grid_copy.start()
            if b + 1 < blocks:
                fetch(b + 1)
        rows = pl.ds((b * fan + e) * CHUNK, CHUNK)
        known = half[b * CHUNK : (b + 1) * CHUNK, :].astype(jnp.float32)
        return silu_half(known + dot(hot[rows, :], table[...]))

    work = [(b, e) for b in range(blocks) for e in range(fan)]
    hidden = first(*work[0])
    w2_copy.wait()
    for k, (b, e) in enumerate(work):
        later = first(*work[k + 1]) if k + 1 < len(work) else None
        center, scale = center_scale(dot(hidden, w2[...]))
        message = center * scale if e == 0 else message + center * scale
        hidden = later
        if e == fan - 1:
            if b == 0:
                grid_copy.wait()
            part = pl.ds(b * CHUNK, CHUNK)
            result[part, :] = (
                grid[part, :].astype(jnp.float32) + message * gain_ref[...]
            ).astype(jnp.bfloat16)
            stream(result, out_ref, out_sems, b, CHUNK).start()
    for b in range(blocks):
        stream(result, out_ref, out_sems, b, CHUNK).wait()


def whole(array):
    return pl.BlockSpec(array.shape, lambda *_: (0,) * array.ndim, pipeline_mode=pl.Buffered(1))


def layer(k, width):
    return pl.BlockSpec((1, width, width), lambda *_: (k, 0, 0), pipeline_mode=pl.Buffered(1))


def params(mib):
    return pltpu.CompilerParams(vmem_limit_bytes=mib * 1024 * 1024)


def on_device(
    nodes,
    edges,
    senders,
    receivers,
    levels,
    counts,
    edge_w1,
    level_bias,
    edge_w2,
    edge_gain,
    node_w1,
    node_w2,
    node_gain,
    grid,
    send_rows,
    dec_index,
    dec_w1,
    dec_w2,
    dec_gain,
):
    bf16, f32 = jnp.bfloat16, jnp.float32
    block, width = nodes.shape
    row_size, col_size = lax.axis_size("row"), lax.axis_size("col")
    slots = edges.shape[2]
    peers, per_peer = send_rows.shape[1:]
    cells, fan = dec_index.shape
    recv_count = block * col_size
    rows = edges.reshape(slots, width)

    send_own, recv_copies = pl.pallas_call(
        project_kernel,
        grid=(1,),
        in_specs=[whole(nodes), layer(1, width), layer(2, width)],
        out_specs=(
            pl.BlockSpec((block, width), lambda i: (0, 0)),
            pl.BlockSpec((col_size, block, width), lambda i: (0, 0, 0)),
        ),
        out_shape=(
            jax.ShapeDtypeStruct((block, width), bf16),
            jax.ShapeDtypeStruct((col_size, block, width), bf16),
        ),
        compiler_params=params(57),
        name="project",
    )(nodes, edge_w1, edge_w1)
    recv_table = lax.all_to_all(recv_copies, "col", 0, 0, tiled=True).reshape(-1, width)
    own = lax.axis_index("row")
    send_pair = lax.ppermute(send_own, "row", [(i, i ^ 1) for i in range(row_size)])
    near = jnp.where(
        own % 2 == 0,
        jnp.concatenate([send_own, send_pair]),
        jnp.concatenate([send_pair, send_own]),
    )
    rows_first, near = lax.optimization_barrier((rows, near))
    far = [
        lax.ppermute(near, "row", [(i, (i + 2 * k) % row_size) for i in range(row_size)])
        for k in range(1, row_size // 2)
    ]
    steps = slots // EDGE_ROWS
    parts = EDGE_ROWS // LANES
    level_ids = levels.reshape(steps, parts, LANES)
    vmem, hbm = pl.BlockSpec(memory_space=pltpu.VMEM), pl.BlockSpec(memory_space=pltpu.HBM)
    edge_half = pl.pallas_call(
        edge_first_kernel,
        in_specs=[vmem, hbm, hbm, vmem],
        out_specs=hbm,
        out_shape=jax.ShapeDtypeStruct((slots, width), bf16),
        scratch_shapes=[
            pltpu.VMEM((slots, width), bf16),
            pltpu.VMEM((slots, width), bf16),
            pltpu.VMEM((width, width), bf16),
            pltpu.SemaphoreType.DMA((steps,)),
            pltpu.SemaphoreType.DMA((steps,)),
            pltpu.SemaphoreType.DMA,
        ],
        compiler_params=params(57),
        cost_estimate=pl.CostEstimate(
            flops=2 * slots * width * width, bytes_accessed=2 * slots * width, transcendentals=0
        ),
        name="edge_first",
    )(level_ids, rows_first, edge_w1, level_bias)

    edge_ids = jnp.concatenate(
        [ids.reshape(steps, parts, LANES) for ids in (senders, receivers)], axis=1
    )
    place = jnp.stack([counts[0, 0], own // 2])
    gain = edge_gain.reshape(1, width)
    smem = pl.BlockSpec(memory_space=pltpu.SMEM)
    edges_out, partial_sum = pl.pallas_call(
        edge_kernel,
        in_specs=[smem, vmem, hbm, hbm] + [vmem] * (4 + len(far)),
        out_specs=(hbm, vmem),
        out_shape=(
            jax.ShapeDtypeStruct((slots, width), bf16),
            jax.ShapeDtypeStruct((recv_count, width), bf16),
        ),
        scratch_shapes=[
            pltpu.VMEM((recv_count, width), f32),
            pltpu.VMEM((block * row_size + recv_count, width), bf16),
            pltpu.VMEM((EDGE_ROWS, width), bf16),
            pltpu.VMEM((slots, width), bf16),
            pltpu.VMEM((slots, width), bf16),
            pltpu.SemaphoreType.DMA((steps,)),
            pltpu.SemaphoreType.DMA((steps,)),
            pltpu.SemaphoreType.DMA((steps,)),
        ],
        compiler_params=params(50),
        name="edges",
    )(place, edge_ids, rows, edge_half, near, *far, recv_table, edge_w2, gain)

    node_parts = lax.all_to_all(
        partial_sum.reshape(col_size, block, width), "col", 0, 0, tiled=True
    )
    strips = per_peer * width // LANES
    picks = send_rows[0].T
    node_scale = node_gain.reshape(1, width)
    nodes_out, picked = pl.pallas_call(
        node_kernel,
        grid=(1,),
        in_specs=[
            whole(node_parts),
            whole(nodes),
            whole(node_w1),
            whole(node_w2),
            whole(node_scale),
            layer(1, width),
            whole(picks),
        ],
        out_specs=(
            pl.BlockSpec((block, width), lambda i: (0, 0)),
            pl.BlockSpec((peers, strips, LANES), lambda i: (0, 0, 0)),
        ),
        out_shape=(
            jax.ShapeDtypeStruct((block, width), bf16),
            jax.ShapeDtypeStruct((peers, strips, LANES), bf16),
        ),
        scratch_shapes=[pltpu.VMEM((peers * strips, LANES), f32)],
        compiler_params=params(12),
        name="nodes",
    )(node_parts, nodes, node_w1, node_w2, node_scale, dec_w1, picks)

    received = lax.all_to_all(picked, ("row", "col"), 0, 0, tiled=True)
    dec_scale = dec_gain.reshape(1, width)
    dec_blocks = cells // CHUNK
    grid_half, dec_hot = pl.pallas_call(
        grid_first_kernel,
        grid=(1,),
        in_specs=[pl.BlockSpec((fan * cells // LANES, LANES), lambda i: (0, 0)), whole(grid), layer(0, width)],
        out_specs=(
            pl.BlockSpec((cells, width), lambda i: (0, 0)),
            pl.BlockSpec((fan * cells, peers * per_peer), lambda i: (0, 0)),
        ),
        out_shape=(
            jax.ShapeDtypeStruct((cells, width), bf16),
            jax.ShapeDtypeStruct((fan * cells, peers * per_peer), bf16),
        ),
        compiler_params=params(57),
        cost_estimate=pl.CostEstimate(
            flops=2 * cells * width * width, bytes_accessed=6 * cells * width, transcendentals=0
        ),
        name="grid_first",
    )(dec_index.T.reshape(-1, LANES), grid, dec_w1)
    grid_out = pl.pallas_call(
        decode_kernel,
        in_specs=[hbm] * 5 + [vmem],
        out_specs=hbm,
        out_shape=jax.ShapeDtypeStruct((cells, width), bf16),
        scratch_shapes=[
            pltpu.VMEM(received.shape, bf16),
            pltpu.VMEM(dec_w2.shape, bf16),
            pltpu.VMEM(dec_hot.shape, bf16),
            pltpu.VMEM(grid_half.shape, bf16),
            pltpu.VMEM(grid.shape, bf16),
            pltpu.VMEM((peers * strips, LANES), f32),
            pltpu.VMEM((peers * per_peer, width), bf16),
            pltpu.VMEM((cells, width), bf16),
            pltpu.SemaphoreType.DMA((3,)),
            pltpu.SemaphoreType.DMA((dec_blocks,)),
            pltpu.SemaphoreType.DMA((dec_blocks,)),
            pltpu.SemaphoreType.DMA((dec_blocks,)),
        ],
        compiler_params=params(53),
        name="decoder",
    )(dec_hot, grid, grid_half, received, dec_w2, dec_scale)
    return (nodes_out, edges_out.reshape(edges.shape), grid_out)


def solution(mesh):
    tile = P("row", "col", None)
    split = P(("row", "col"), None)
    return jax.shard_map(
        on_device,
        mesh=mesh,
        in_specs=(
            split,
            P("row", "col", None, None),
            tile,
            tile,
            tile,
            P("row", "col"),
            P(),
            P(),
            P(),
            P(),
            P(),
            P(),
            P(),
            split,
            P(("row", "col"), None, None),
            split,
            P(),
            P(),
            P(),
        ),
        out_specs=(split, P("row", "col", None, None), split),
        check_vma=False,
    )
```

```python
import jax
import jax.numpy as jnp
from jax import lax
from jax.experimental import pallas as pl
from jax.experimental.pallas import tpu as pltpu
from jax.sharding import PartitionSpec as P

EPSILON = 1e-05
LANES = 128
EDGE_ROWS = 1024
CHUNK = 256
AHEAD = 2


def dot(a, b):
    return jnp.dot(a, b, preferred_element_type=jnp.float32)


def silu_half(half):
    return (half + half * jnp.tanh(half)).astype(jnp.bfloat16)


def center_scale(values):
    center = values - jnp.mean(values, axis=-1, keepdims=True)
    spread = jnp.mean(center * center, axis=-1, keepdims=True)
    return center, lax.rsqrt(spread + EPSILON)


def column_hot(ids, count):
    lanes = lax.broadcasted_iota(jnp.int32, (ids.shape[0], count), 1)
    return (ids == lanes).astype(jnp.bfloat16)


def stacked_hot(columns, first, number, count):
    return jnp.concatenate(
        [column_hot(columns[:, p : p + 1], count) for p in range(first, first + number)], axis=0
    )


def row_hot(ids, count):
    rows = lax.broadcasted_iota(jnp.int32, (count, ids.shape[1]), 0)
    return (ids == rows).astype(jnp.bfloat16)


def project_kernel(nodes_ref, send_weight_ref, recv_weight_ref, send_ref, recv_ref):
    nodes = nodes_ref[...]
    recv = (0.5 * dot(nodes, recv_weight_ref[0])).astype(jnp.bfloat16)
    for k in range(recv_ref.shape[0]):
        recv_ref[k] = recv
    send_ref[...] = (0.5 * dot(nodes, send_weight_ref[0])).astype(jnp.bfloat16)


def edge_first_kernel(
    ids_ref, rows_ref, w1_ref, bias_ref, half_ref, rows, half, weight, row_sems, half_sems, weight_sem
):
    blocks = ids_ref.shape[0]
    span = ids_ref.shape[1] * LANES
    weight_copy = pltpu.make_async_copy(w1_ref.at[0], weight, weight_sem)
    weight_copy.start()
    copies = [
        pltpu.make_async_copy(
            rows_ref.at[pl.ds(k * span, span)], rows.at[pl.ds(k * span, span)], row_sems.at[k]
        )
        for k in range(blocks)
    ]
    for copy in copies[:AHEAD]:
        copy.start()
    weight_copy.wait()
    outs = []
    for k in range(blocks):
        columns = jnp.transpose(ids_ref[k])
        hot = stacked_hot(columns, 0, ids_ref.shape[1], bias_ref.shape[0])
        copies[k].wait()
        if k + AHEAD < blocks:
            copies[k + AHEAD].start()
        part = slice(k * span, (k + 1) * span)
        product = dot(rows[part, :], weight[...]) + dot(hot, bias_ref[...])
        half[part, :] = (0.5 * product).astype(jnp.bfloat16)
        place = pl.ds(k * span, span)
        outs.append(pltpu.make_async_copy(half.at[place], half_ref.at[place], half_sems.at[k]))
        outs[-1].start()
    for out in outs:
        out.wait()


def edge_kernel(
    place_ref,
    ids_ref,
    rows_ref,
    half_ref,
    near_ref,
    far1_ref,
    far2_ref,
    far3_ref,
    recv_ref,
    w2_ref,
    gain_ref,
    out_ref,
    sum_ref,
    total,
    table,
    messages,
    edge_rows,
    half,
    row_sems,
    half_sems,
    out_sems,
):
    blocks = ids_ref.shape[0]
    parts = ids_ref.shape[1] // 2
    rows = parts * LANES
    count, chip = place_ref[0], place_ref[1]
    send_count = table.shape[0] - recv_ref.shape[0]

    def stream(source, target, sems, k):
        place = pl.ds(pl.multiple_of(k * rows, rows), rows)
        return pltpu.make_async_copy(source.at[place], target.at[place], sems.at[k])

    for k in range(blocks):
        stream(half_ref, half, half_sems, k).start()
        stream(rows_ref, edge_rows, row_sems, k).start()
    total[...] = jnp.zeros_like(total)
    sources = (near_ref, far1_ref, far2_ref, far3_ref)
    span = near_ref.shape[0]
    for k, source in enumerate(sources):
        owner = lax.rem(chip - k + len(sources), len(sources))
        table[pl.ds(pl.multiple_of(owner * span, span), span), :] = source[...]
    table[send_count:, :] = recv_ref[...]

    @pl.loop(0, blocks)
    def _(step):
        base = pl.multiple_of(step * rows, rows)

        stream(half_ref, half, half_sems, step).wait()
        stream(rows_ref, edge_rows, row_sems, step).wait()

        @pl.when(base >= count)
        def _():
            stream(edge_rows, out_ref, out_sems, step).start()

        @pl.when(base < count)
        def _():
            ids = ids_ref[step]
            columns = jnp.transpose(ids)

            def first(c):
                hot = jnp.concatenate(
                    [
                        stacked_hot(columns, c * CHUNK // LANES, CHUNK // LANES, send_count),
                        stacked_hot(
                            columns, parts + c * CHUNK // LANES, CHUNK // LANES, recv_ref.shape[0]
                        ),
                    ],
                    axis=1,
                )
                known = half[pl.ds(base + c * CHUNK, CHUNK), :].astype(jnp.float32)
                return silu_half(known + dot(hot, table[...]))

            def second(c, hidden):
                center, scale = center_scale(dot(hidden, w2_ref[...]))
                slot = base + c * CHUNK + lax.broadcasted_iota(jnp.int32, (CHUNK, 1), 0)
                scale = jnp.where(slot < count, scale, 0.0)
                message = (center * scale * gain_ref[...]).astype(jnp.bfloat16)
                messages[c * CHUNK : (c + 1) * CHUNK, :] = message
                place = pl.ds(base + c * CHUNK, CHUNK)
                edge_rows[place, :] = (
                    edge_rows[place, :].astype(jnp.float32) + message.astype(jnp.float32)
                ).astype(jnp.bfloat16)

            hidden = first(0)
            for c in range(rows // CHUNK):
                later = first(c + 1) if (c + 1) * CHUNK < rows else None
                second(c, hidden)
                hidden = later
            stream(edge_rows, out_ref, out_sems, step).start()
            spread_hot = jnp.concatenate(
                [
                    row_hot(ids[parts + p : parts + p + 1, :], recv_ref.shape[0])
                    for p in range(parts)
                ],
                axis=1,
            )
            total[...] += dot(spread_hot, messages[...])

    sum_ref[...] = total[...].astype(jnp.bfloat16)
    for k in range(blocks):
        stream(edge_rows, out_ref, out_sems, k).wait()


def grid_first_kernel(grid_ref, w1_ref, w2_ref, half_ref, centered_ref):
    half_ref[...] = (0.5 * dot(grid_ref[...], w1_ref[0])).astype(jnp.bfloat16)
    w2 = w2_ref[...].astype(jnp.float32)
    centered_ref[...] = (w2 - jnp.mean(w2, axis=-1, keepdims=True)).astype(jnp.bfloat16)


def node_kernel(
    parts_ref, nodes_ref, w1_ref, w2_ref, gain_ref, dec_w1_ref, picks_ref, out_ref, picked_ref, wide
):
    low = jnp.sum(parts_ref[...].astype(jnp.float32), axis=0).astype(jnp.bfloat16)
    nodes = nodes_ref[...]
    pre = dot(nodes, w1_ref[0]) + dot(low, w1_ref[1])
    center, scale = center_scale(dot(silu_half(0.5 * pre), w2_ref[...]))
    fresh = (nodes.astype(jnp.float32) + center * scale * gain_ref[...]).astype(jnp.bfloat16)
    out_ref[...] = fresh
    projected = (0.5 * dot(fresh, dec_w1_ref[0])).astype(jnp.bfloat16)
    peers, strips, _ = picked_ref.shape
    columns = jnp.transpose(picks_ref[...])
    groups = strips // picks_ref.shape[0]
    for j in range(picks_ref.shape[0]):
        chosen = dot(column_hot(columns[:, j : j + 1], nodes.shape[0]), projected)
        for q in range(groups):
            wide[pl.ds(j * groups + q, peers, stride=strips), :] = chosen[
                :, q * LANES : (q + 1) * LANES
            ]
    picked_ref[...] = wide[...].reshape(picked_ref.shape).astype(jnp.bfloat16)


def decode_kernel(
    ids_ref,
    grid_ref,
    half_ref,
    received_ref,
    w2_ref,
    gain_ref,
    out_ref,
    received,
    w2,
    half,
    grid,
    wide,
    table,
    result,
    sems,
    out_sems,
):
    cells = grid_ref.shape[0]
    blocks = cells // CHUNK
    fan = ids_ref.shape[0] * LANES // cells
    peers, strips, _ = received_ref.shape
    groups = table.shape[1] // LANES
    per_peer = strips // groups
    pairs = ((received_ref, received), (half_ref, half), (w2_ref, w2), (grid_ref, grid))
    copies = [
        pltpu.make_async_copy(source, target, sems.at[k])
        for k, (source, target) in enumerate(pairs)
    ]
    for copy in copies:
        copy.start()

    span = cells // out_sems.shape[0]
    outs = [
        pltpu.make_async_copy(
            result.at[pl.ds(k * span, span)], out_ref.at[pl.ds(k * span, span)], out_sems.at[k]
        )
        for k in range(out_sems.shape[0])
    ]
    copies[0].wait()
    wide[...] = received[...].astype(jnp.float32).reshape(wide.shape)
    for j in range(per_peer):
        for q in range(groups):
            table[j * peers : (j + 1) * peers, q * LANES : (q + 1) * LANES] = wide[
                pl.ds(j * groups + q, peers, stride=strips), :
            ].astype(jnp.bfloat16)
    ids = ids_ref[...]
    columns = jnp.transpose(lax.rem(ids, per_peer) * peers + lax.div(ids, per_peer))
    for copy in copies[1:]:
        copy.wait()

    def first(b, e):
        parts = CHUNK // LANES
        hot = stacked_hot(columns, e * (cells // LANES) + b * parts, parts, table.shape[0])
        known = half[b * CHUNK : (b + 1) * CHUNK, :].astype(jnp.float32)
        return silu_half(known + dot(hot, table[...]))

    work = [(b, e) for b in range(blocks) for e in range(fan)]
    hidden = first(*work[0])
    for k, (b, e) in enumerate(work):
        later = first(*work[k + 1]) if k + 1 < len(work) else None
        center = dot(hidden, w2[...])
        spread = jnp.mean(center * center, axis=-1, keepdims=True)
        scaled = center * lax.rsqrt(spread + EPSILON)
        message = scaled if e == 0 else message + scaled
        hidden = later
        if e == fan - 1:
            part = slice(b * CHUNK, (b + 1) * CHUNK)
            result[part, :] = (
                grid[part, :].astype(jnp.float32) + message * gain_ref[...]
            ).astype(jnp.bfloat16)
            if (b + 1) * CHUNK % span == 0:
                outs[(b + 1) * CHUNK // span - 1].start()
    for out in outs:
        out.wait()


def whole(array):
    return pl.BlockSpec(array.shape, lambda *_: (0,) * array.ndim, pipeline_mode=pl.Buffered(1))


def layer(k, width):
    return pl.BlockSpec((1, width, width), lambda *_: (k, 0, 0), pipeline_mode=pl.Buffered(1))


def params(mib):
    return pltpu.CompilerParams(vmem_limit_bytes=mib * 1024 * 1024)


def on_device(
    nodes,
    edges,
    senders,
    receivers,
    levels,
    counts,
    edge_w1,
    level_bias,
    edge_w2,
    edge_gain,
    node_w1,
    node_w2,
    node_gain,
    grid,
    send_rows,
    dec_index,
    dec_w1,
    dec_w2,
    dec_gain,
):
    bf16, f32 = jnp.bfloat16, jnp.float32
    block, width = nodes.shape
    row_size, col_size = lax.axis_size("row"), lax.axis_size("col")
    slots = edges.shape[2]
    peers, per_peer = send_rows.shape[1:]
    cells, fan = dec_index.shape
    recv_count = block * col_size
    rows = edges.reshape(slots, width)

    send_own, recv_copies = pl.pallas_call(
        project_kernel,
        grid=(1,),
        in_specs=[whole(nodes), layer(1, width), layer(2, width)],
        out_specs=(
            pl.BlockSpec((block, width), lambda i: (0, 0)),
            pl.BlockSpec((col_size, block, width), lambda i: (0, 0, 0)),
        ),
        out_shape=(
            jax.ShapeDtypeStruct((block, width), bf16),
            jax.ShapeDtypeStruct((col_size, block, width), bf16),
        ),
        compiler_params=params(57),
        name="project",
    )(nodes, edge_w1, edge_w1)
    recv_table = lax.all_to_all(recv_copies, "col", 0, 0, tiled=True).reshape(-1, width)
    own = lax.axis_index("row")
    send_pair = lax.ppermute(send_own, "row", [(i, i ^ 1) for i in range(row_size)])
    near = jnp.where(
        own % 2 == 0,
        jnp.concatenate([send_own, send_pair]),
        jnp.concatenate([send_pair, send_own]),
    )
    rows_first, near = lax.optimization_barrier((rows, near))
    far = [
        lax.ppermute(near, "row", [(i, (i + 2 * k) % row_size) for i in range(row_size)])
        for k in range(1, row_size // 2)
    ]
    steps = slots // EDGE_ROWS
    parts = EDGE_ROWS // LANES
    level_ids = levels.reshape(steps, parts, LANES)
    vmem, hbm = pl.BlockSpec(memory_space=pltpu.VMEM), pl.BlockSpec(memory_space=pltpu.HBM)
    edge_half = pl.pallas_call(
        edge_first_kernel,
        in_specs=[vmem, hbm, hbm, vmem],
        out_specs=hbm,
        out_shape=jax.ShapeDtypeStruct((slots, width), bf16),
        scratch_shapes=[
            pltpu.VMEM((slots, width), bf16),
            pltpu.VMEM((slots, width), bf16),
            pltpu.VMEM((width, width), bf16),
            pltpu.SemaphoreType.DMA((steps,)),
            pltpu.SemaphoreType.DMA((steps,)),
            pltpu.SemaphoreType.DMA,
        ],
        compiler_params=params(57),
        cost_estimate=pl.CostEstimate(
            flops=2 * slots * width * width, bytes_accessed=2 * slots * width, transcendentals=0
        ),
        name="edge_first",
    )(level_ids, rows_first, edge_w1, level_bias)

    edge_ids = jnp.concatenate(
        [ids.reshape(steps, parts, LANES) for ids in (senders, receivers)], axis=1
    )
    place = jnp.stack([counts[0, 0], own // 2])
    gain = edge_gain.reshape(1, width)
    smem = pl.BlockSpec(memory_space=pltpu.SMEM)
    edges_out, partial_sum = pl.pallas_call(
        edge_kernel,
        in_specs=[smem, vmem, hbm, hbm] + [vmem] * (4 + len(far)),
        out_specs=(hbm, vmem),
        out_shape=(
            jax.ShapeDtypeStruct((slots, width), bf16),
            jax.ShapeDtypeStruct((recv_count, width), bf16),
        ),
        scratch_shapes=[
            pltpu.VMEM((recv_count, width), f32),
            pltpu.VMEM((block * row_size + recv_count, width), bf16),
            pltpu.VMEM((EDGE_ROWS, width), bf16),
            pltpu.VMEM((slots, width), bf16),
            pltpu.VMEM((slots, width), bf16),
            pltpu.SemaphoreType.DMA((steps,)),
            pltpu.SemaphoreType.DMA((steps,)),
            pltpu.SemaphoreType.DMA((steps,)),
        ],
        compiler_params=params(50),
        name="edges",
    )(place, edge_ids, rows, edge_half, near, *far, recv_table, edge_w2, gain)

    node_parts = lax.all_to_all(
        partial_sum.reshape(col_size, block, width), "col", 0, 0, tiled=True
    )
    strips = per_peer * width // LANES
    picks = send_rows[0].T
    node_scale = node_gain.reshape(1, width)
    nodes_out, picked = pl.pallas_call(
        node_kernel,
        grid=(1,),
        in_specs=[
            whole(node_parts),
            whole(nodes),
            whole(node_w1),
            whole(node_w2),
            whole(node_scale),
            layer(1, width),
            whole(picks),
        ],
        out_specs=(
            pl.BlockSpec((block, width), lambda i: (0, 0)),
            pl.BlockSpec((peers, strips, LANES), lambda i: (0, 0, 0)),
        ),
        out_shape=(
            jax.ShapeDtypeStruct((block, width), bf16),
            jax.ShapeDtypeStruct((peers, strips, LANES), bf16),
        ),
        scratch_shapes=[pltpu.VMEM((peers * strips, LANES), f32)],
        compiler_params=params(12),
        name="nodes",
    )(node_parts, nodes, node_w1, node_w2, node_scale, dec_w1, picks)

    received = lax.all_to_all(picked, ("row", "col"), 0, 0, tiled=True)
    dec_scale = dec_gain.reshape(1, width)
    grid_half, dec_centered = pl.pallas_call(
        grid_first_kernel,
        grid=(1,),
        in_specs=[whole(grid), layer(0, width), whole(dec_w2)],
        out_specs=(
            pl.BlockSpec((cells, width), lambda i: (0, 0)),
            pl.BlockSpec((width, width), lambda i: (0, 0)),
        ),
        out_shape=(
            jax.ShapeDtypeStruct((cells, width), bf16),
            jax.ShapeDtypeStruct((width, width), bf16),
        ),
        compiler_params=params(57),
        cost_estimate=pl.CostEstimate(
            flops=2 * cells * width * width, bytes_accessed=6 * cells * width, transcendentals=0
        ),
        name="grid_first",
    )(grid, dec_w1, dec_w2)
    grid_out = pl.pallas_call(
        decode_kernel,
        in_specs=[vmem] + [hbm] * 4 + [vmem],
        out_specs=hbm,
        out_shape=jax.ShapeDtypeStruct((cells, width), bf16),
        scratch_shapes=[
            pltpu.VMEM(received.shape, bf16),
            pltpu.VMEM(dec_w2.shape, bf16),
            pltpu.VMEM(grid_half.shape, bf16),
            pltpu.VMEM(grid.shape, bf16),
            pltpu.VMEM((peers * strips, LANES), f32),
            pltpu.VMEM((peers * per_peer, width), bf16),
            pltpu.VMEM((cells, width), bf16),
            pltpu.SemaphoreType.DMA((4,)),
            pltpu.SemaphoreType.DMA((2,)),
        ],
        compiler_params=params(53),
        name="decoder",
    )(dec_index.T.reshape(-1, LANES), grid, grid_half, received, dec_centered, dec_scale)
    return (nodes_out, edges_out.reshape(edges.shape), grid_out)


def solution(mesh):
    tile = P("row", "col", None)
    split = P(("row", "col"), None)
    return jax.shard_map(
        on_device,
        mesh=mesh,
        in_specs=(
            split,
            P("row", "col", None, None),
            tile,
            tile,
            tile,
            P("row", "col"),
            P(),
            P(),
            P(),
            P(),
            P(),
            P(),
            P(),
            split,
            P(("row", "col"), None, None),
            split,
            P(),
            P(),
            P(),
        ),
        out_specs=(split, P("row", "col", None, None), split),
        check_vma=False,
    )
```

```python
import jax
import jax.numpy as jnp
from jax import lax
from jax.experimental import pallas as pl
from jax.experimental.pallas import tpu as pltpu
from jax.sharding import PartitionSpec as P

EPSILON = 1e-05
LANES = 128
EDGE_ROWS = 1024
CHUNK = 256
AHEAD = 2


def dot(a, b):
    return jnp.dot(a, b, preferred_element_type=jnp.float32)


def silu_half(half):
    return (half + half * jnp.tanh(half)).astype(jnp.bfloat16)


def center_scale(values):
    center = values - jnp.mean(values, axis=-1, keepdims=True)
    spread = jnp.mean(center * center, axis=-1, keepdims=True)
    return center, lax.rsqrt(spread + EPSILON)


def column_hot(ids, count):
    one, zero = jnp.ones((), jnp.bfloat16), jnp.zeros((), jnp.bfloat16)
    if count % LANES:
        lanes = lax.broadcasted_iota(jnp.int32, (ids.shape[0], count), 1)
        return (ids == lanes).astype(jnp.bfloat16)
    shape = (ids.shape[0], LANES)
    lane = lax.broadcasted_iota(jnp.int32, shape, 1).astype(jnp.float32).astype(jnp.bfloat16)
    low = jnp.broadcast_to((ids & (LANES - 1)).astype(jnp.float32).astype(jnp.bfloat16), shape)
    high = jnp.broadcast_to(lax.div(ids, LANES).astype(jnp.float32).astype(jnp.bfloat16), shape)
    hit = jnp.where(low == lane, one, zero)
    return jnp.concatenate(
        [
            jnp.where(high == jnp.asarray(strip, jnp.bfloat16), hit, zero)
            for strip in range(count // LANES)
        ],
        axis=1,
    )


def stacked_hot(columns, first, number, count):
    return jnp.concatenate(
        [column_hot(columns[:, p : p + 1], count) for p in range(first, first + number)], axis=0
    )


def row_hot(ids, count):
    rows = lax.broadcasted_iota(jnp.int16, (count, ids.shape[1]), 0)
    one, zero = jnp.ones((), jnp.bfloat16), jnp.zeros((), jnp.bfloat16)
    return jnp.where(ids.astype(jnp.int16) == rows, one, zero)


def project_kernel(nodes_ref, send_weight_ref, recv_weight_ref, send_ref, recv_ref):
    nodes = nodes_ref[...]
    recv = (0.5 * dot(nodes, recv_weight_ref[0])).astype(jnp.bfloat16)
    for k in range(recv_ref.shape[0]):
        recv_ref[k] = recv
    send_ref[...] = (0.5 * dot(nodes, send_weight_ref[0])).astype(jnp.bfloat16)


def edge_first_kernel(
    ids_ref, rows_ref, w1_ref, bias_ref, half_ref, rows, half, weight, row_sems, half_sems, weight_sem
):
    blocks = ids_ref.shape[0]
    span = ids_ref.shape[1] * LANES
    weight_copy = pltpu.make_async_copy(w1_ref.at[0], weight, weight_sem)
    weight_copy.start()
    copies = [
        pltpu.make_async_copy(
            rows_ref.at[pl.ds(k * span, span)], rows.at[pl.ds(k * span, span)], row_sems.at[k]
        )
        for k in range(blocks)
    ]
    for copy in copies[:AHEAD]:
        copy.start()
    weight_copy.wait()
    outs = []
    for k in range(blocks):
        columns = jnp.transpose(ids_ref[k])
        hot = stacked_hot(columns, 0, ids_ref.shape[1], bias_ref.shape[0])
        copies[k].wait()
        if k + AHEAD < blocks:
            copies[k + AHEAD].start()
        part = slice(k * span, (k + 1) * span)
        product = dot(rows[part, :], weight[...]) + dot(hot, bias_ref[...])
        half[part, :] = (0.5 * product).astype(jnp.bfloat16)
        place = pl.ds(k * span, span)
        outs.append(pltpu.make_async_copy(half.at[place], half_ref.at[place], half_sems.at[k]))
        outs[-1].start()
    for out in outs:
        out.wait()


def edge_kernel(
    place_ref,
    ids_ref,
    rows_ref,
    half_ref,
    near_ref,
    far1_ref,
    far2_ref,
    far3_ref,
    recv_ref,
    w2_ref,
    gain_ref,
    out_ref,
    sum_ref,
    total,
    table,
    messages,
    edge_rows,
    half,
    row_sems,
    half_sems,
    out_sems,
):
    blocks = ids_ref.shape[0]
    parts = ids_ref.shape[1] // 2
    rows = parts * LANES
    count, chip = place_ref[0], place_ref[1]
    send_count = table.shape[0] - recv_ref.shape[0]

    def stream(source, target, sems, k):
        place = pl.ds(pl.multiple_of(k * rows, rows), rows)
        return pltpu.make_async_copy(source.at[place], target.at[place], sems.at[k])

    for k in range(blocks):
        stream(half_ref, half, half_sems, k).start()
        stream(rows_ref, edge_rows, row_sems, k).start()
    total[...] = jnp.zeros_like(total)
    sources = (near_ref, far1_ref, far2_ref, far3_ref)
    span = near_ref.shape[0]
    for k, source in enumerate(sources):
        owner = lax.rem(chip - k + len(sources), len(sources))
        table[pl.ds(pl.multiple_of(owner * span, span), span), :] = source[...]
    table[send_count:, :] = recv_ref[...]

    @pl.loop(0, blocks)
    def _(step):
        base = pl.multiple_of(step * rows, rows)

        stream(half_ref, half, half_sems, step).wait()
        stream(rows_ref, edge_rows, row_sems, step).wait()

        @pl.when(base >= count)
        def _():
            stream(edge_rows, out_ref, out_sems, step).start()

        @pl.when(base < count)
        def _():
            ids = ids_ref[step]
            columns = jnp.transpose(ids)

            def first(c):
                hot = jnp.concatenate(
                    [
                        stacked_hot(columns, c * CHUNK // LANES, CHUNK // LANES, send_count),
                        stacked_hot(
                            columns, parts + c * CHUNK // LANES, CHUNK // LANES, recv_ref.shape[0]
                        ),
                    ],
                    axis=1,
                )
                known = half[pl.ds(base + c * CHUNK, CHUNK), :].astype(jnp.float32)
                return silu_half(known + dot(hot, table[...]))

            def second(c, hidden):
                center, scale = center_scale(dot(hidden, w2_ref[...]))
                slot = base + c * CHUNK + lax.broadcasted_iota(jnp.int32, (CHUNK, 1), 0)
                scale = jnp.where(slot < count, scale, 0.0)
                message = (center * scale * gain_ref[...]).astype(jnp.bfloat16)
                messages[c * CHUNK : (c + 1) * CHUNK, :] = message
                place = pl.ds(base + c * CHUNK, CHUNK)
                edge_rows[place, :] = (
                    edge_rows[place, :].astype(jnp.float32) + message.astype(jnp.float32)
                ).astype(jnp.bfloat16)

            hidden = first(0)
            for c in range(rows // CHUNK):
                later = first(c + 1) if (c + 1) * CHUNK < rows else None
                second(c, hidden)
                hidden = later
            stream(edge_rows, out_ref, out_sems, step).start()
            spread_hot = jnp.concatenate(
                [
                    row_hot(ids[parts + p : parts + p + 1, :], recv_ref.shape[0])
                    for p in range(parts)
                ],
                axis=1,
            )
            total[...] += dot(spread_hot, messages[...])

    sum_ref[...] = total[...].astype(jnp.bfloat16)
    for k in range(blocks):
        stream(edge_rows, out_ref, out_sems, k).wait()


def grid_first_kernel(grid_ref, w1_ref, w2_ref, half_ref, centered_ref):
    half_ref[...] = (0.5 * dot(grid_ref[...], w1_ref[0])).astype(jnp.bfloat16)
    w2 = w2_ref[...].astype(jnp.float32)
    centered_ref[...] = (w2 - jnp.mean(w2, axis=-1, keepdims=True)).astype(jnp.bfloat16)


def node_kernel(
    parts_ref, nodes_ref, w1_ref, w2_ref, gain_ref, dec_w1_ref, picks_ref, out_ref, picked_ref, wide
):
    low = jnp.sum(parts_ref[...].astype(jnp.float32), axis=0).astype(jnp.bfloat16)
    nodes = nodes_ref[...]
    pre = dot(nodes, w1_ref[0]) + dot(low, w1_ref[1])
    center, scale = center_scale(dot(silu_half(0.5 * pre), w2_ref[...]))
    fresh = (nodes.astype(jnp.float32) + center * scale * gain_ref[...]).astype(jnp.bfloat16)
    out_ref[...] = fresh
    projected = (0.5 * dot(fresh, dec_w1_ref[0])).astype(jnp.bfloat16)
    peers, strips, _ = picked_ref.shape
    columns = jnp.transpose(picks_ref[...])
    groups = strips // picks_ref.shape[0]
    for j in range(picks_ref.shape[0]):
        chosen = dot(column_hot(columns[:, j : j + 1], nodes.shape[0]), projected)
        for q in range(groups):
            wide[pl.ds(j * groups + q, peers, stride=strips), :] = chosen[
                :, q * LANES : (q + 1) * LANES
            ]
    picked_ref[...] = wide[...].reshape(picked_ref.shape).astype(jnp.bfloat16)


def decode_kernel(
    ids_ref,
    grid_ref,
    half_ref,
    received_ref,
    w2_ref,
    gain_ref,
    out_ref,
    received,
    w2,
    half,
    grid,
    wide,
    table,
    result,
    sems,
    out_sems,
):
    cells = grid_ref.shape[0]
    blocks = cells // CHUNK
    fan = ids_ref.shape[0] * LANES // cells
    peers, strips, _ = received_ref.shape
    groups = table.shape[1] // LANES
    per_peer = strips // groups
    pairs = ((received_ref, received), (half_ref, half), (w2_ref, w2), (grid_ref, grid))
    copies = [
        pltpu.make_async_copy(source, target, sems.at[k])
        for k, (source, target) in enumerate(pairs)
    ]
    for copy in copies:
        copy.start()

    span = cells // out_sems.shape[0]
    outs = [
        pltpu.make_async_copy(
            result.at[pl.ds(k * span, span)], out_ref.at[pl.ds(k * span, span)], out_sems.at[k]
        )
        for k in range(out_sems.shape[0])
    ]
    copies[0].wait()
    wide[...] = received[...].astype(jnp.float32).reshape(wide.shape)
    for j in range(per_peer):
        for q in range(groups):
            table[j * peers : (j + 1) * peers, q * LANES : (q + 1) * LANES] = wide[
                pl.ds(j * groups + q, peers, stride=strips), :
            ].astype(jnp.bfloat16)
    ids = ids_ref[...]
    columns = jnp.transpose(lax.rem(ids, per_peer) * peers + lax.div(ids, per_peer))
    for copy in copies[1:]:
        copy.wait()

    def first(b, e):
        parts = CHUNK // LANES
        hot = stacked_hot(columns, e * (cells // LANES) + b * parts, parts, table.shape[0])
        known = half[b * CHUNK : (b + 1) * CHUNK, :].astype(jnp.float32)
        return silu_half(known + dot(hot, table[...]))

    work = [(b, e) for b in range(blocks) for e in range(fan)]
    hidden = first(*work[0])
    for k, (b, e) in enumerate(work):
        later = first(*work[k + 1]) if k + 1 < len(work) else None
        center = dot(hidden, w2[...])
        spread = jnp.mean(center * center, axis=-1, keepdims=True)
        scaled = center * lax.rsqrt(spread + EPSILON)
        message = scaled if e == 0 else message + scaled
        hidden = later
        if e == fan - 1:
            part = slice(b * CHUNK, (b + 1) * CHUNK)
            result[part, :] = (
                grid[part, :].astype(jnp.float32) + message * gain_ref[...]
            ).astype(jnp.bfloat16)
            if (b + 1) * CHUNK % span == 0:
                outs[(b + 1) * CHUNK // span - 1].start()
    for out in outs:
        out.wait()


def whole(array):
    return pl.BlockSpec(array.shape, lambda *_: (0,) * array.ndim, pipeline_mode=pl.Buffered(1))


def layer(k, width):
    return pl.BlockSpec((1, width, width), lambda *_: (k, 0, 0), pipeline_mode=pl.Buffered(1))


def params(mib):
    return pltpu.CompilerParams(vmem_limit_bytes=mib * 1024 * 1024)


def on_device(
    nodes,
    edges,
    senders,
    receivers,
    levels,
    counts,
    edge_w1,
    level_bias,
    edge_w2,
    edge_gain,
    node_w1,
    node_w2,
    node_gain,
    grid,
    send_rows,
    dec_index,
    dec_w1,
    dec_w2,
    dec_gain,
):
    bf16, f32 = jnp.bfloat16, jnp.float32
    block, width = nodes.shape
    row_size, col_size = lax.axis_size("row"), lax.axis_size("col")
    slots = edges.shape[2]
    peers, per_peer = send_rows.shape[1:]
    cells, fan = dec_index.shape
    recv_count = block * col_size
    rows = edges.reshape(slots, width)

    send_own, recv_copies = pl.pallas_call(
        project_kernel,
        grid=(1,),
        in_specs=[whole(nodes), layer(1, width), layer(2, width)],
        out_specs=(
            pl.BlockSpec((block, width), lambda i: (0, 0)),
            pl.BlockSpec((col_size, block, width), lambda i: (0, 0, 0)),
        ),
        out_shape=(
            jax.ShapeDtypeStruct((block, width), bf16),
            jax.ShapeDtypeStruct((col_size, block, width), bf16),
        ),
        compiler_params=params(57),
        name="project",
    )(nodes, edge_w1, edge_w1)
    recv_table = lax.all_to_all(recv_copies, "col", 0, 0, tiled=True).reshape(-1, width)
    own = lax.axis_index("row")
    send_pair = lax.ppermute(send_own, "row", [(i, i ^ 1) for i in range(row_size)])
    near = jnp.where(
        own % 2 == 0,
        jnp.concatenate([send_own, send_pair]),
        jnp.concatenate([send_pair, send_own]),
    )
    rows_first, near = lax.optimization_barrier((rows, near))
    far = [
        lax.ppermute(near, "row", [(i, (i + 2 * k) % row_size) for i in range(row_size)])
        for k in range(1, row_size // 2)
    ]
    steps = slots // EDGE_ROWS
    parts = EDGE_ROWS // LANES
    level_ids = levels.reshape(steps, parts, LANES)
    vmem, hbm = pl.BlockSpec(memory_space=pltpu.VMEM), pl.BlockSpec(memory_space=pltpu.HBM)
    edge_half = pl.pallas_call(
        edge_first_kernel,
        in_specs=[vmem, hbm, hbm, vmem],
        out_specs=hbm,
        out_shape=jax.ShapeDtypeStruct((slots, width), bf16),
        scratch_shapes=[
            pltpu.VMEM((slots, width), bf16),
            pltpu.VMEM((slots, width), bf16),
            pltpu.VMEM((width, width), bf16),
            pltpu.SemaphoreType.DMA((steps,)),
            pltpu.SemaphoreType.DMA((steps,)),
            pltpu.SemaphoreType.DMA,
        ],
        compiler_params=params(57),
        cost_estimate=pl.CostEstimate(
            flops=2 * slots * width * width, bytes_accessed=2 * slots * width, transcendentals=0
        ),
        name="edge_first",
    )(level_ids, rows_first, edge_w1, level_bias)

    edge_ids = jnp.concatenate(
        [ids.reshape(steps, parts, LANES) for ids in (senders, receivers)], axis=1
    )
    place = jnp.stack([counts[0, 0], own // 2])
    gain = edge_gain.reshape(1, width)
    smem = pl.BlockSpec(memory_space=pltpu.SMEM)
    edges_out, partial_sum = pl.pallas_call(
        edge_kernel,
        in_specs=[smem, vmem, hbm, hbm] + [vmem] * (4 + len(far)),
        out_specs=(hbm, vmem),
        out_shape=(
            jax.ShapeDtypeStruct((slots, width), bf16),
            jax.ShapeDtypeStruct((recv_count, width), bf16),
        ),
        scratch_shapes=[
            pltpu.VMEM((recv_count, width), f32),
            pltpu.VMEM((block * row_size + recv_count, width), bf16),
            pltpu.VMEM((EDGE_ROWS, width), bf16),
            pltpu.VMEM((slots, width), bf16),
            pltpu.VMEM((slots, width), bf16),
            pltpu.SemaphoreType.DMA((steps,)),
            pltpu.SemaphoreType.DMA((steps,)),
            pltpu.SemaphoreType.DMA((steps,)),
        ],
        compiler_params=params(50),
        name="edges",
    )(place, edge_ids, rows, edge_half, near, *far, recv_table, edge_w2, gain)

    node_parts = lax.all_to_all(
        partial_sum.reshape(col_size, block, width), "col", 0, 0, tiled=True
    )
    strips = per_peer * width // LANES
    picks = send_rows[0].T
    node_scale = node_gain.reshape(1, width)
    nodes_out, picked = pl.pallas_call(
        node_kernel,
        grid=(1,),
        in_specs=[
            whole(node_parts),
            whole(nodes),
            whole(node_w1),
            whole(node_w2),
            whole(node_scale),
            layer(1, width),
            whole(picks),
        ],
        out_specs=(
            pl.BlockSpec((block, width), lambda i: (0, 0)),
            pl.BlockSpec((peers, strips, LANES), lambda i: (0, 0, 0)),
        ),
        out_shape=(
            jax.ShapeDtypeStruct((block, width), bf16),
            jax.ShapeDtypeStruct((peers, strips, LANES), bf16),
        ),
        scratch_shapes=[pltpu.VMEM((peers * strips, LANES), f32)],
        compiler_params=params(12),
        name="nodes",
    )(node_parts, nodes, node_w1, node_w2, node_scale, dec_w1, picks)

    received = lax.all_to_all(picked, ("row", "col"), 0, 0, tiled=True)
    dec_scale = dec_gain.reshape(1, width)
    grid_half, dec_centered = pl.pallas_call(
        grid_first_kernel,
        grid=(1,),
        in_specs=[whole(grid), layer(0, width), whole(dec_w2)],
        out_specs=(
            pl.BlockSpec((cells, width), lambda i: (0, 0)),
            pl.BlockSpec((width, width), lambda i: (0, 0)),
        ),
        out_shape=(
            jax.ShapeDtypeStruct((cells, width), bf16),
            jax.ShapeDtypeStruct((width, width), bf16),
        ),
        compiler_params=params(57),
        cost_estimate=pl.CostEstimate(
            flops=2 * cells * width * width, bytes_accessed=6 * cells * width, transcendentals=0
        ),
        name="grid_first",
    )(grid, dec_w1, dec_w2)
    grid_out = pl.pallas_call(
        decode_kernel,
        in_specs=[vmem] + [hbm] * 4 + [vmem],
        out_specs=hbm,
        out_shape=jax.ShapeDtypeStruct((cells, width), bf16),
        scratch_shapes=[
            pltpu.VMEM(received.shape, bf16),
            pltpu.VMEM(dec_w2.shape, bf16),
            pltpu.VMEM(grid_half.shape, bf16),
            pltpu.VMEM(grid.shape, bf16),
            pltpu.VMEM((peers * strips, LANES), f32),
            pltpu.VMEM((peers * per_peer, width), bf16),
            pltpu.VMEM((cells, width), bf16),
            pltpu.SemaphoreType.DMA((4,)),
            pltpu.SemaphoreType.DMA((2,)),
        ],
        compiler_params=params(53),
        name="decoder",
    )(dec_index.T.reshape(-1, LANES), grid, grid_half, received, dec_centered, dec_scale)
    return (nodes_out, edges_out.reshape(edges.shape), grid_out)


def solution(mesh):
    tile = P("row", "col", None)
    split = P(("row", "col"), None)
    return jax.shard_map(
        on_device,
        mesh=mesh,
        in_specs=(
            split,
            P("row", "col", None, None),
            tile,
            tile,
            tile,
            P("row", "col"),
            P(),
            P(),
            P(),
            P(),
            P(),
            P(),
            P(),
            split,
            P(("row", "col"), None, None),
            split,
            P(),
            P(),
            P(),
        ),
        out_specs=(split, P("row", "col", None, None), split),
        check_vma=False,
    )
```

```python
import jax
import jax.numpy as jnp
from jax import lax
from jax.experimental import pallas as pl
from jax.experimental.pallas import tpu as pltpu
from jax.sharding import PartitionSpec as P

EPSILON = 1e-05
LANES = 128
EDGE_ROWS = 1024
CHUNK = 256
AHEAD = 2


def dot(a, b):
    return jnp.dot(a, b, preferred_element_type=jnp.float32)


def silu_half(half):
    return (half + half * jnp.tanh(half)).astype(jnp.bfloat16)


def center_scale(values):
    center = values - jnp.mean(values, axis=-1, keepdims=True)
    spread = jnp.mean(center * center, axis=-1, keepdims=True)
    return center, lax.rsqrt(spread + EPSILON)


def column_hot(ids, count):
    one, zero = jnp.ones((), jnp.bfloat16), jnp.zeros((), jnp.bfloat16)
    if count % LANES:
        lanes = lax.broadcasted_iota(jnp.int32, (ids.shape[0], count), 1)
        return (ids == lanes).astype(jnp.bfloat16)
    shape = (ids.shape[0], LANES)
    lane = lax.broadcasted_iota(jnp.int32, shape, 1).astype(jnp.float32).astype(jnp.bfloat16)
    low = jnp.broadcast_to((ids & (LANES - 1)).astype(jnp.float32).astype(jnp.bfloat16), shape)
    high = jnp.broadcast_to(lax.div(ids, LANES).astype(jnp.float32).astype(jnp.bfloat16), shape)
    hit = jnp.where(low == lane, one, zero)
    return jnp.concatenate(
        [
            jnp.where(high == jnp.asarray(strip, jnp.bfloat16), hit, zero)
            for strip in range(count // LANES)
        ],
        axis=1,
    )


def stacked_hot(columns, first, number, count):
    return jnp.concatenate(
        [column_hot(columns[:, p : p + 1], count) for p in range(first, first + number)], axis=0
    )


def row_hot(ids, count):
    rows = lax.broadcasted_iota(jnp.int16, (count, ids.shape[1]), 0)
    one, zero = jnp.ones((), jnp.bfloat16), jnp.zeros((), jnp.bfloat16)
    return jnp.where(ids.astype(jnp.int16) == rows, one, zero)


def project_kernel(nodes_ref, send_weight_ref, recv_weight_ref, send_ref, recv_ref):
    nodes = nodes_ref[...]
    recv = (0.5 * dot(nodes, recv_weight_ref[0])).astype(jnp.bfloat16)
    for k in range(recv_ref.shape[0]):
        recv_ref[k] = recv
    send_ref[...] = (0.5 * dot(nodes, send_weight_ref[0])).astype(jnp.bfloat16)


def edge_first_kernel(
    ids_ref, rows_ref, w1_ref, bias_ref, half_ref, rows, half, weight, row_sems, half_sems, weight_sem
):
    blocks = ids_ref.shape[0]
    span = ids_ref.shape[1] * LANES
    weight_copy = pltpu.make_async_copy(w1_ref.at[0], weight, weight_sem)
    weight_copy.start()
    copies = [
        pltpu.make_async_copy(
            rows_ref.at[pl.ds(k * span, span)], rows.at[pl.ds(k * span, span)], row_sems.at[k]
        )
        for k in range(blocks)
    ]
    for copy in copies[:AHEAD]:
        copy.start()
    levels, width = bias_ref.shape
    bias = bias_ref[...].astype(jnp.float32)
    bias = jnp.concatenate([bias, jnp.zeros((LANES - levels, width), jnp.float32)], axis=0)
    weight_copy.wait()
    joined = jnp.concatenate([weight[...], bias.astype(jnp.bfloat16)], axis=0)
    outs = []
    for k in range(blocks):
        columns = jnp.transpose(ids_ref[k])
        hot = stacked_hot(columns, 0, ids_ref.shape[1], LANES)
        copies[k].wait()
        if k + AHEAD < blocks:
            copies[k + AHEAD].start()
        part = slice(k * span, (k + 1) * span)
        product = dot(jnp.concatenate([rows[part, :], hot], axis=1), joined)
        half[part, :] = (0.5 * product).astype(jnp.bfloat16)
        place = pl.ds(k * span, span)
        outs.append(pltpu.make_async_copy(half.at[place], half_ref.at[place], half_sems.at[k]))
        outs[-1].start()
    for out in outs:
        out.wait()


def edge_kernel(
    place_ref,
    ids_ref,
    rows_ref,
    half_ref,
    near_ref,
    far1_ref,
    far2_ref,
    far3_ref,
    recv_ref,
    w2_ref,
    gain_ref,
    out_ref,
    sum_ref,
    total,
    table,
    messages,
    edge_rows,
    half,
    row_sems,
    half_sems,
    out_sems,
):
    blocks = ids_ref.shape[0]
    parts = ids_ref.shape[1] // 2
    rows = parts * LANES
    count, chip = place_ref[0], place_ref[1]
    send_count = table.shape[0] - recv_ref.shape[0]

    def stream(source, target, sems, k):
        place = pl.ds(pl.multiple_of(k * rows, rows), rows)
        return pltpu.make_async_copy(source.at[place], target.at[place], sems.at[k])

    for k in range(blocks):
        stream(half_ref, half, half_sems, k).start()
        stream(rows_ref, edge_rows, row_sems, k).start()
    total[...] = jnp.zeros_like(total)
    sources = (near_ref, far1_ref, far2_ref, far3_ref)
    span = near_ref.shape[0]
    for k, source in enumerate(sources):
        owner = lax.rem(chip - k + len(sources), len(sources))
        table[pl.ds(pl.multiple_of(owner * span, span), span), :] = source[...]
    table[send_count:, :] = recv_ref[...]

    @pl.loop(0, blocks)
    def _(step):
        base = pl.multiple_of(step * rows, rows)

        stream(half_ref, half, half_sems, step).wait()
        stream(rows_ref, edge_rows, row_sems, step).wait()

        @pl.when(base >= count)
        def _():
            stream(edge_rows, out_ref, out_sems, step).start()

        @pl.when(base < count)
        def _():
            ids = ids_ref[step]
            columns = jnp.transpose(ids)

            def first(c):
                hot = jnp.concatenate(
                    [
                        stacked_hot(columns, c * CHUNK // LANES, CHUNK // LANES, send_count),
                        stacked_hot(
                            columns, parts + c * CHUNK // LANES, CHUNK // LANES, recv_ref.shape[0]
                        ),
                    ],
                    axis=1,
                )
                known = half[pl.ds(base + c * CHUNK, CHUNK), :].astype(jnp.float32)
                return silu_half(known + dot(hot, table[...]))

            def second(c, hidden):
                center, scale = center_scale(dot(hidden, w2_ref[...]))
                slot = base + c * CHUNK + lax.broadcasted_iota(jnp.int32, (CHUNK, 1), 0)
                scale = jnp.where(slot < count, scale, 0.0)
                message = (center * scale * gain_ref[...]).astype(jnp.bfloat16)
                messages[c * CHUNK : (c + 1) * CHUNK, :] = message
                place = pl.ds(base + c * CHUNK, CHUNK)
                edge_rows[place, :] = (
                    edge_rows[place, :].astype(jnp.float32) + message.astype(jnp.float32)
                ).astype(jnp.bfloat16)

            hidden = first(0)
            for c in range(rows // CHUNK):
                later = first(c + 1) if (c + 1) * CHUNK < rows else None
                second(c, hidden)
                hidden = later
            stream(edge_rows, out_ref, out_sems, step).start()
            spread_hot = jnp.concatenate(
                [
                    row_hot(ids[parts + p : parts + p + 1, :], recv_ref.shape[0])
                    for p in range(parts)
                ],
                axis=1,
            )
            total[...] += dot(spread_hot, messages[...])

    sum_ref[...] = total[...].astype(jnp.bfloat16)
    for k in range(blocks):
        stream(edge_rows, out_ref, out_sems, k).wait()


def grid_first_kernel(grid_ref, w1_ref, w2_ref, half_ref, centered_ref):
    half_ref[...] = (0.5 * dot(grid_ref[...], w1_ref[0])).astype(jnp.bfloat16)
    w2 = w2_ref[...].astype(jnp.float32)
    centered_ref[...] = (w2 - jnp.mean(w2, axis=-1, keepdims=True)).astype(jnp.bfloat16)


def node_kernel(
    parts_ref,
    nodes_ref,
    w1_ref,
    w2_ref,
    gain_ref,
    dec_w1_ref,
    picks_ref,
    out_ref,
    picked_ref,
    wide,
    picked,
    sems,
):
    low = jnp.sum(parts_ref[...].astype(jnp.float32), axis=0).astype(jnp.bfloat16)
    nodes = nodes_ref[...]
    pre = dot(nodes, w1_ref[0]) + dot(low, w1_ref[1])
    center, scale = center_scale(dot(silu_half(0.5 * pre), w2_ref[...]))
    fresh = (nodes.astype(jnp.float32) + center * scale * gain_ref[...]).astype(jnp.bfloat16)
    out_ref[...] = fresh
    projected = (0.5 * dot(fresh, dec_w1_ref[0])).astype(jnp.bfloat16)
    peers, strips, _ = picked_ref.shape
    columns = jnp.transpose(picks_ref[...])
    groups = strips // picks_ref.shape[0]
    span = peers // sems.shape[0]
    copies = []
    for h in range(sems.shape[0]):
        for j in range(picks_ref.shape[0]):
            ids = columns[h * span : (h + 1) * span, j : j + 1]
            chosen = dot(column_hot(ids, nodes.shape[0]), projected)
            for q in range(groups):
                wide[pl.ds(h * span * strips + j * groups + q, span, stride=strips), :] = chosen[
                    :, q * LANES : (q + 1) * LANES
                ]
        half = wide[h * span * strips : (h + 1) * span * strips, :]
        place = pl.ds(h * span, span)
        picked[place] = half.reshape(span, strips, LANES).astype(jnp.bfloat16)
        copies.append(pltpu.make_async_copy(picked.at[place], picked_ref.at[place], sems.at[h]))
        copies[-1].start()
    for copy in copies:
        copy.wait()


def decode_kernel(
    ids_ref,
    grid_ref,
    half_ref,
    received_ref,
    w2_ref,
    gain_ref,
    out_ref,
    received,
    w2,
    half,
    grid,
    wide,
    table,
    result,
    sems,
    out_sems,
):
    cells = grid_ref.shape[0]
    blocks = cells // CHUNK
    fan = ids_ref.shape[0] * LANES // cells
    peers, strips, _ = received_ref.shape
    groups = table.shape[1] // LANES
    per_peer = strips // groups
    pairs = ((received_ref, received), (half_ref, half), (w2_ref, w2), (grid_ref, grid))
    copies = [
        pltpu.make_async_copy(source, target, sems.at[k])
        for k, (source, target) in enumerate(pairs)
    ]
    for copy in copies:
        copy.start()

    span = cells // out_sems.shape[0]
    outs = [
        pltpu.make_async_copy(
            result.at[pl.ds(k * span, span)], out_ref.at[pl.ds(k * span, span)], out_sems.at[k]
        )
        for k in range(out_sems.shape[0])
    ]
    copies[0].wait()
    wide[...] = received[...].astype(jnp.float32).reshape(wide.shape)
    for j in range(per_peer):
        for q in range(groups):
            table[j * peers : (j + 1) * peers, q * LANES : (q + 1) * LANES] = wide[
                pl.ds(j * groups + q, peers, stride=strips), :
            ].astype(jnp.bfloat16)
    ids = ids_ref[...]
    columns = jnp.transpose(lax.rem(ids, per_peer) * peers + lax.div(ids, per_peer))
    for copy in copies[1:]:
        copy.wait()

    def first(b, e):
        parts = CHUNK // LANES
        hot = stacked_hot(columns, e * (cells // LANES) + b * parts, parts, table.shape[0])
        known = half[b * CHUNK : (b + 1) * CHUNK, :].astype(jnp.float32)
        return silu_half(known + dot(hot, table[...]))

    work = [(b, e) for b in range(blocks) for e in range(fan)]
    hidden = first(*work[0])
    for k, (b, e) in enumerate(work):
        later = first(*work[k + 1]) if k + 1 < len(work) else None
        center = dot(hidden, w2[...])
        spread = jnp.mean(center * center, axis=-1, keepdims=True)
        scaled = center * lax.rsqrt(spread + EPSILON)
        message = scaled if e == 0 else message + scaled
        hidden = later
        if e == fan - 1:
            part = slice(b * CHUNK, (b + 1) * CHUNK)
            result[part, :] = (
                grid[part, :].astype(jnp.float32) + message * gain_ref[...]
            ).astype(jnp.bfloat16)
            if (b + 1) * CHUNK % span == 0:
                outs[(b + 1) * CHUNK // span - 1].start()
    for out in outs:
        out.wait()


def whole(array):
    return pl.BlockSpec(array.shape, lambda *_: (0,) * array.ndim, pipeline_mode=pl.Buffered(1))


def layer(k, width):
    return pl.BlockSpec((1, width, width), lambda *_: (k, 0, 0), pipeline_mode=pl.Buffered(1))


def params(mib):
    return pltpu.CompilerParams(vmem_limit_bytes=mib * 1024 * 1024)


def on_device(
    nodes,
    edges,
    senders,
    receivers,
    levels,
    counts,
    edge_w1,
    level_bias,
    edge_w2,
    edge_gain,
    node_w1,
    node_w2,
    node_gain,
    grid,
    send_rows,
    dec_index,
    dec_w1,
    dec_w2,
    dec_gain,
):
    bf16, f32 = jnp.bfloat16, jnp.float32
    block, width = nodes.shape
    row_size, col_size = lax.axis_size("row"), lax.axis_size("col")
    slots = edges.shape[2]
    peers, per_peer = send_rows.shape[1:]
    cells, fan = dec_index.shape
    recv_count = block * col_size
    rows = edges.reshape(slots, width)

    send_own, recv_copies = pl.pallas_call(
        project_kernel,
        grid=(1,),
        in_specs=[whole(nodes), layer(1, width), layer(2, width)],
        out_specs=(
            pl.BlockSpec((block, width), lambda i: (0, 0)),
            pl.BlockSpec((col_size, block, width), lambda i: (0, 0, 0)),
        ),
        out_shape=(
            jax.ShapeDtypeStruct((block, width), bf16),
            jax.ShapeDtypeStruct((col_size, block, width), bf16),
        ),
        compiler_params=params(57),
        name="project",
    )(nodes, edge_w1, edge_w1)
    recv_table = lax.all_to_all(recv_copies, "col", 0, 0, tiled=True).reshape(-1, width)
    own = lax.axis_index("row")
    send_pair = lax.ppermute(send_own, "row", [(i, i ^ 1) for i in range(row_size)])
    near = jnp.where(
        own % 2 == 0,
        jnp.concatenate([send_own, send_pair]),
        jnp.concatenate([send_pair, send_own]),
    )
    rows_first, near = lax.optimization_barrier((rows, near))
    far = [
        lax.ppermute(near, "row", [(i, (i + 2 * k) % row_size) for i in range(row_size)])
        for k in range(1, row_size // 2)
    ]
    steps = slots // EDGE_ROWS
    parts = EDGE_ROWS // LANES
    level_ids = levels.reshape(steps, parts, LANES)
    vmem, hbm = pl.BlockSpec(memory_space=pltpu.VMEM), pl.BlockSpec(memory_space=pltpu.HBM)
    edge_half = pl.pallas_call(
        edge_first_kernel,
        in_specs=[vmem, hbm, hbm, vmem],
        out_specs=hbm,
        out_shape=jax.ShapeDtypeStruct((slots, width), bf16),
        scratch_shapes=[
            pltpu.VMEM((slots, width), bf16),
            pltpu.VMEM((slots, width), bf16),
            pltpu.VMEM((width, width), bf16),
            pltpu.SemaphoreType.DMA((steps,)),
            pltpu.SemaphoreType.DMA((steps,)),
            pltpu.SemaphoreType.DMA,
        ],
        compiler_params=params(57),
        cost_estimate=pl.CostEstimate(
            flops=2 * slots * width * width, bytes_accessed=2 * slots * width, transcendentals=0
        ),
        name="edge_first",
    )(level_ids, rows_first, edge_w1, level_bias)

    edge_ids = jnp.concatenate(
        [ids.reshape(steps, parts, LANES) for ids in (senders, receivers)], axis=1
    )
    place = jnp.stack([counts[0, 0], own // 2])
    gain = edge_gain.reshape(1, width)
    smem = pl.BlockSpec(memory_space=pltpu.SMEM)
    edges_out, partial_sum = pl.pallas_call(
        edge_kernel,
        in_specs=[smem, vmem, hbm, hbm] + [vmem] * (4 + len(far)),
        out_specs=(hbm, vmem),
        out_shape=(
            jax.ShapeDtypeStruct((slots, width), bf16),
            jax.ShapeDtypeStruct((recv_count, width), bf16),
        ),
        scratch_shapes=[
            pltpu.VMEM((recv_count, width), f32),
            pltpu.VMEM((block * row_size + recv_count, width), bf16),
            pltpu.VMEM((EDGE_ROWS, width), bf16),
            pltpu.VMEM((slots, width), bf16),
            pltpu.VMEM((slots, width), bf16),
            pltpu.SemaphoreType.DMA((steps,)),
            pltpu.SemaphoreType.DMA((steps,)),
            pltpu.SemaphoreType.DMA((steps,)),
        ],
        compiler_params=params(50),
        name="edges",
    )(place, edge_ids, rows, edge_half, near, *far, recv_table, edge_w2, gain)

    node_parts = lax.all_to_all(
        partial_sum.reshape(col_size, block, width), "col", 0, 0, tiled=True
    )
    strips = per_peer * width // LANES
    picks = send_rows[0].T
    node_scale = node_gain.reshape(1, width)
    nodes_out, picked = pl.pallas_call(
        node_kernel,
        grid=(1,),
        in_specs=[
            whole(node_parts),
            whole(nodes),
            whole(node_w1),
            whole(node_w2),
            whole(node_scale),
            layer(1, width),
            whole(picks),
        ],
        out_specs=(
            pl.BlockSpec((block, width), lambda i: (0, 0)),
            hbm,
        ),
        out_shape=(
            jax.ShapeDtypeStruct((block, width), bf16),
            jax.ShapeDtypeStruct((peers, strips, LANES), bf16),
        ),
        scratch_shapes=[
            pltpu.VMEM((peers * strips, LANES), f32),
            pltpu.VMEM((peers, strips, LANES), bf16),
            pltpu.SemaphoreType.DMA((2,)),
        ],
        compiler_params=params(12),
        name="nodes",
    )(node_parts, nodes, node_w1, node_w2, node_scale, dec_w1, picks)

    received = lax.all_to_all(picked, ("row", "col"), 0, 0, tiled=True)
    dec_scale = dec_gain.reshape(1, width)
    grid_half, dec_centered = pl.pallas_call(
        grid_first_kernel,
        grid=(1,),
        in_specs=[whole(grid), layer(0, width), whole(dec_w2)],
        out_specs=(
            pl.BlockSpec((cells, width), lambda i: (0, 0)),
            pl.BlockSpec((width, width), lambda i: (0, 0)),
        ),
        out_shape=(
            jax.ShapeDtypeStruct((cells, width), bf16),
            jax.ShapeDtypeStruct((width, width), bf16),
        ),
        compiler_params=params(57),
        cost_estimate=pl.CostEstimate(
            flops=2 * cells * width * width, bytes_accessed=6 * cells * width, transcendentals=0
        ),
        name="grid_first",
    )(grid, dec_w1, dec_w2)
    grid_out = pl.pallas_call(
        decode_kernel,
        in_specs=[vmem] + [hbm] * 4 + [vmem],
        out_specs=hbm,
        out_shape=jax.ShapeDtypeStruct((cells, width), bf16),
        scratch_shapes=[
            pltpu.VMEM(received.shape, bf16),
            pltpu.VMEM(dec_w2.shape, bf16),
            pltpu.VMEM(grid_half.shape, bf16),
            pltpu.VMEM(grid.shape, bf16),
            pltpu.VMEM((peers * strips, LANES), f32),
            pltpu.VMEM((peers * per_peer, width), bf16),
            pltpu.VMEM((cells, width), bf16),
            pltpu.SemaphoreType.DMA((4,)),
            pltpu.SemaphoreType.DMA((2,)),
        ],
        compiler_params=params(53),
        name="decoder",
    )(dec_index.T.reshape(-1, LANES), grid, grid_half, received, dec_centered, dec_scale)
    return (nodes_out, edges_out.reshape(edges.shape), grid_out)


def solution(mesh):
    tile = P("row", "col", None)
    split = P(("row", "col"), None)
    return jax.shard_map(
        on_device,
        mesh=mesh,
        in_specs=(
            split,
            P("row", "col", None, None),
            tile,
            tile,
            tile,
            P("row", "col"),
            P(),
            P(),
            P(),
            P(),
            P(),
            P(),
            P(),
            split,
            P(("row", "col"), None, None),
            split,
            P(),
            P(),
            P(),
        ),
        out_specs=(split, P("row", "col", None, None), split),
        check_vma=False,
    )
```
